32 devices in a mesh: mp: 4 (over x, core), fsdp: 8 (over z, y).
Axes of the slice: x: 2, y: 2, z: 4, core: 2. Of those that a mesh axis runs over, the one named last changes fastest.
Arguments:
- activations: bfloat16 [4, 1024, 8192], P('mp', 'fsdp'), may hold values from -6 to 6
- out_grads: bfloat16 [4, 1024, 7168], P('mp', 'fsdp'), may hold values from -0.29882812 to 0.29882812
- seq_ids: int32 [4, 1024], P('mp', 'fsdp'), may hold values from 0 to 1, as said below
- weights: bfloat16 [4, 32768, 1792], P('mp', 'fsdp'), may hold values from -6 to 6
Outputs:
- merged: bfloat16 [32768, 1792], P('fsdp')
The draws below stay inside these ranges and needn't reach their ends.
Inputs may be any that keep to these rules, and one draw needn't show every extreme that they name: `seq_ids`: sequence ids never fall along the tokens of a copy; in every copy one of the 2 sequences holds exactly 768 neighbouring tokens and the other the remaining 1024 - 768, in either order.
All inputs are finite; a program needn't handle non-finite values.
Results may differ from the reference program's by a relative error of at most 0.001.
Values may be sent and summed in bfloat16 or wider, within the bound.
No kernel may reach another device: no remote copies, remote signals or barrier semaphores. Data moves between devices by JAX's collectives and lax.ppermute only.
A program may use at most 192 MiB of HBM per device.

```python
import jax
import jax.numpy as jnp
from jax import lax

D = 8192
F = 7168
FB = 4
SEQS = 2
TOKENS = 1024
MOST = 768
COPIES = 4
N_MP = 4


def draw_seq_ids(key, part):
    order = jax.random.randint(jax.random.fold_in(key, 11), (COPIES,), 0, 2).astype(jnp.int32)
    first_len = jnp.where(order == 1, jnp.int32(MOST), jnp.int32(TOKENS - MOST)).astype(jnp.int32)
    position = jnp.arange(TOKENS, dtype=jnp.int32)
    return (position[None, :] >= first_len[:, None]).astype(jnp.int32)


def block_scale(stream_key, shape, cuts, least, largest):
    def one(dim, blocks):
        heights = jax.random.uniform(jax.random.fold_in(jax.random.fold_in(stream_key, 6), dim), (blocks,), jnp.float32, least / len(cuts), largest / len(cuts))
        return jnp.repeat(jnp.exp(heights), shape[dim] // blocks).reshape((-1,) + (1,) * (len(shape) - dim - 1))

    factor_of = one(*cuts[0])
    for cut in cuts[1:]:
        factor_of = factor_of * one(*cut)
    return factor_of


def centred(rng, shape, scale, most, cuts=(), kind=jnp.bfloat16):
    result = scale * jax.random.normal(rng, shape, jnp.float32)
    if cuts:
        result = result * block_scale(rng, shape, cuts, -0.22, 0.18)
    return jnp.clip(result, -most, most).astype(kind)


def setup_inputs(seed: int = 0) -> dict:
    keys = jax.random.split(jax.random.key(seed), 5)
    activations = centred(keys[0], (COPIES, TOKENS, D), 1.0, 6.0, ((0, 4), (1, 8)))
    out_grads = centred(keys[1], (COPIES, TOKENS, F), 0.05, 0.29882812, ((0, 4), (1, 8)))
    seq_ids = draw_seq_ids(jax.random.fold_in(keys[4], 71), 0)
    weights = centred(keys[3], (COPIES, FB * D, F // FB), 1.0, 6.0, ((0, 4), (1, 8)))
    return {"activations": activations, "out_grads": out_grads, "seq_ids": seq_ids, "weights": weights}


smoothing = 0.05


def restack(full):
    rows, cols = full.shape
    return full.reshape(rows, FB, cols // FB).transpose(1, 0, 2).reshape(FB * rows, cols // FB)


def fisher_of(acts, grads, owners):
    total = acts.shape[0]
    xs = acts.astype(jnp.float32)
    gs = grads.astype(jnp.float32)
    fisher = jnp.zeros((acts.shape[1], grads.shape[1]), jnp.float32)
    for seq in range(SEQS):
        first = jnp.sum((owners < seq).astype(jnp.int32)).astype(jnp.int32)
        first = jnp.minimum(first, jnp.int32(total - MOST)).astype(jnp.int32)
        xw = lax.dynamic_slice_in_dim(xs, first, MOST, 0)
        gw = lax.dynamic_slice_in_dim(gs, first, MOST, 0)
        iw = lax.dynamic_slice_in_dim(owners, first, MOST, 0)
        masked = jnp.where((iw == seq)[:, None], gw, jnp.zeros_like(gw))
        grad = jnp.dot(xw.T, masked, precision=lax.Precision.HIGHEST)
        fisher = fisher + grad * grad
    return fisher / SEQS


def reference(activations, out_grads, seq_ids, weights):
    numer = jnp.zeros(weights.shape[1:], jnp.float32)
    denom = jnp.zeros(weights.shape[1:], jnp.float32)
    for copy in range(N_MP):
        prior = restack(fisher_of(activations[copy], out_grads[copy], seq_ids[copy])) + smoothing
        numer = numer + prior * weights[copy].astype(jnp.float32)
        denom = denom + prior
    return (numer / denom).astype(jnp.bfloat16)
```

```python
import functools

import jax
import jax.numpy as jnp
from jax import lax
from jax.experimental import pallas as pl
from jax.experimental.pallas import tpu as pltpu
from jax.sharding import PartitionSpec as P

F = 7168
SEQS = 2
CHUNKS = 2
COL_TILE = 256
ROW_TILE = 256

smoothing = 0.05


def merge_kernel(copies, shards, place_ref, slot_ref, *refs):
    own = refs[0]
    low = refs[1:shards]
    high = refs[shards:2 * shards - 1]
    refs = refs[2 * shards - 1:]
    grads = refs[:copies]
    weights = refs[copies:2 * copies]
    out_ref, acts, sem = refs[2 * copies:]
    rows, tok = own.shape[1], own.shape[2]
    spread = own.shape[0] // copies
    a = place_ref[0]

    def fetch(source, slot):
        return [
            pltpu.make_async_copy(
                source.at[copy * spread + part],
                acts.at[copy, slot, :, pl.ds(part * tok, tok)],
                sem,
            )
            for copy in range(copies)
            for part in range(spread)
        ]

    @pl.when(pl.program_id(0) == 0)
    def _():
        for copy in fetch(own, 0):
            copy.start()
        for slot in range(1, shards):
            @pl.when(a >= slot)
            def _(slot=slot):
                for copy in fetch(low[slot - 1], slot):
                    copy.start()

            @pl.when(a < slot)
            def _(slot=slot):
                for copy in fetch(high[shards - slot - 1], slot):
                    copy.start()
        pltpu.make_async_copy(acts, acts, sem).wait()

    height = min(ROW_TILE, rows)

    def row_tile(step, carry):
        at = pl.ds(pl.multiple_of(step * height, height), height)
        numer = denom = None
        for copy in range(copies):
            sums = []
            lone = slot_ref[copy]
            for first, count in ((0, 1), (1, shards - 1)):
                total = None
                for offset in range(first, first + count):
                    slot = lax.rem(lone + offset, shards)
                    term = jnp.dot(
                        acts[copy, slot, at, :], grads[copy][slot], preferred_element_type=jnp.float32
                    )
                    total = term if total is None else total + term
                sums.append(total)
            prior = (sums[0] * sums[0] + sums[1] * sums[1]) * (1.0 / SEQS) + smoothing
            term = prior * weights[copy][at, :].astype(jnp.float32)
            numer = term if numer is None else numer + term
            denom = prior if denom is None else denom + prior
        out_ref[at, :] = (numer / denom).astype(out_ref.dtype)
        return carry

    lax.fori_loop(0, rows // height, row_tile, 0)


def merge_rows(place, slots, own, low, high, grads, weights):
    copies, shards = len(grads), grads[0].shape[0]
    tok, width = grads[0].shape[1:]
    rows = own.shape[1]
    return pl.pallas_call(
        functools.partial(merge_kernel, copies, shards),
        out_shape=jax.ShapeDtypeStruct((rows, width), jnp.bfloat16),
        grid_spec=pltpu.PrefetchScalarGridSpec(
            num_scalar_prefetch=2,
            grid=(width // COL_TILE,),
            in_specs=[pl.BlockSpec(memory_space=pl.ANY)] * (2 * shards - 1)
            + [pl.BlockSpec((shards, tok, COL_TILE), lambda j, *_: (0, 0, j))] * copies
            + [pl.BlockSpec((rows, COL_TILE), lambda j, *_: (0, j))] * copies,
            out_specs=pl.BlockSpec((rows, COL_TILE), lambda j, *_: (0, j)),
            scratch_shapes=[
                pltpu.VMEM((copies, shards, rows, tok), jnp.bfloat16),
                pltpu.SemaphoreType.DMA,
            ],
        ),
        compiler_params=pltpu.CompilerParams(vmem_limit_bytes=56 * 1024 * 1024),
        cost_estimate=pl.CostEstimate(
            flops=2 * copies * shards * tok * rows * width,
            bytes_accessed=2 * copies * (shards * tok * (rows + width) + rows * width) + 2 * rows * width,
            transcendentals=0,
        ),
    )(place, slots, own, *low, *high, *grads, *weights)


def per_device(activations, out_grads, seq_ids, weights):
    copies = lax.axis_size("mp")
    devices = lax.axis_size("fsdp")
    rows, width = weights.shape[1:]
    blocks = F // width
    spread = devices // blocks
    tok = activations.shape[1]
    share = rows // copies
    part = share // CHUNKS
    m = lax.axis_index("mp")
    i = lax.axis_index("fsdp")
    a, h = i // spread, i % spread

    def to_copy(value, flip):
        return lax.ppermute(value, "mp", [(s, s ^ flip) for s in range(copies)])

    def to_block(value, shift):
        pairs = [(s, (s // spread + shift) % blocks * spread + s % spread) for s in range(devices)]
        return lax.ppermute(value, "fsdp", pairs)

    def to_half(value, shift):
        pairs = [(s, s // spread * spread + (s % spread + shift) % spread) for s in range(devices)]
        return lax.ppermute(value, "fsdp", pairs)

    def to_plane(value, flip, shift):
        pairs = [
            (c * devices + s, (c ^ flip) * devices + s // spread * spread + (s % spread + shift) % spread)
            for c in range(copies)
            for s in range(devices)
        ]
        return lax.ppermute(value, ("mp", "fsdp"), pairs)

    def along(value, step, direction):
        pairs = [
            (s, s + direction * spread)
            for s in range(devices)
            if 0 <= s // spread + direction < blocks and 0 <= s // spread - direction * (step - 1) < blocks
        ]
        return lax.ppermute(value, "fsdp", pairs)

    mine = jnp.where((a == 1) & (h == 0), seq_ids[0, 0], 0)
    second = lax.psum(jnp.where(jnp.arange(copies) == m, mine, 0), ("mp", "fsdp"))
    alone = jnp.where(second == 1, 0, blocks - 1)[m ^ jnp.arange(copies)]
    slots = ((a - alone) % blocks).astype(jnp.int32)
    place = a.astype(jnp.int32)[None]

    grad_blocks = out_grads[0].reshape(tok, blocks, width).transpose(1, 0, 2)
    grads = [None] * copies
    for flip, value in ((0, grad_blocks), (2, to_copy(grad_blocks, 2))):
        block = [lax.dynamic_index_in_dim(value, (a + k) % blocks, 0, keepdims=False) for k in range(blocks)]
        held = jnp.stack([block[0]] + [to_block(block[k], k) for k in range(1, blocks)])
        held = jnp.concatenate([held] + [to_half(held, d) for d in range(1, spread)], axis=1)
        grads[flip] = held
        grads[flip ^ 1] = to_copy(held, 1)

    acts = activations[0].T.reshape(spread, copies, share, tok)
    shard = []
    for flip in range(copies):
        for d in range(spread):
            piece = lax.dynamic_slice(acts, ((h + d) % spread, m ^ flip, 0, 0), (1, 1, share, tok))[0, 0]
            shard.append(piece if flip == d == 0 else to_plane(piece, flip, d))

    merged = jnp.zeros((rows, width), jnp.bfloat16)
    for chunk in range(CHUNKS):
        cut = slice(chunk * part, (chunk + 1) * part)
        own = jnp.stack([piece[cut] for piece in shard])
        low, high = [], []
        right = left = own
        for step in range(1, blocks):
            right = along(right, step, 1)
            left = along(left, step, -1)
            low.append(right)
            high.append(left)
        held = []
        for flip in range(copies):
            piece = lax.dynamic_slice_in_dim(weights[0], (m ^ flip) * share + chunk * part, part, 0)
            held.append(piece if flip == 0 else to_copy(piece, flip))
        mine = merge_rows(place, slots, own, low, high, grads, held)
        far = to_copy(mine, 2)
        for flip, value in ((0, mine), (1, to_copy(mine, 1)), (2, far), (3, to_copy(far, 1))):
            merged = lax.dynamic_update_slice_in_dim(merged, value, (m ^ flip) * share + chunk * part, 0)
    return merged


def solution(mesh):
    placed = (P("mp", "fsdp", None), P("mp", "fsdp", None), P("mp", "fsdp"), P("mp", "fsdp", None))
    return jax.shard_map(
        per_device, mesh=mesh, in_specs=placed, out_specs=P("fsdp", None), check_vma=False
    )
```

```python
import functools

import jax
import jax.numpy as jnp
from jax import lax
from jax.experimental import pallas as pl
from jax.experimental.pallas import tpu as pltpu
from jax.sharding import PartitionSpec as P

F = 7168
SEQS = 2
CHUNKS = 2
PIECES = 4
COL_TILE = 256
ROW_TILE = 256

smoothing = 0.05


def merge_kernel(copies, shards, place_ref, slot_ref, *refs):
    own = refs[0]
    low = refs[1:shards]
    high = refs[shards:2 * shards - 1]
    refs = refs[2 * shards - 1:]
    grads = refs[:copies]
    weights = refs[copies:2 * copies]
    out_ref, acts, sem = refs[2 * copies:]
    rows, tok = own.shape[1], own.shape[2]
    spread = own.shape[0] // copies
    a = place_ref[0]

    def fetch(source, slot):
        return [
            pltpu.make_async_copy(
                source.at[copy * spread + part],
                acts.at[copy, slot, :, pl.ds(part * tok, tok)],
                sem,
            )
            for copy in range(copies)
            for part in range(spread)
        ]

    @pl.when(pl.program_id(0) == 0)
    def _():
        for copy in fetch(own, 0):
            copy.start()
        for slot in range(1, shards):
            @pl.when(a >= slot)
            def _(slot=slot):
                for copy in fetch(low[slot - 1], slot):
                    copy.start()

            @pl.when(a < slot)
            def _(slot=slot):
                for copy in fetch(high[shards - slot - 1], slot):
                    copy.start()
        pltpu.make_async_copy(acts, acts, sem).wait()

    height = min(ROW_TILE, rows)

    def row_tile(step, carry):
        at = pl.ds(pl.multiple_of(step * height, height), height)
        numer = denom = None
        for copy in range(copies):
            sums = []
            lone = slot_ref[copy]
            for first, count in ((0, 1), (1, shards - 1)):
                total = None
                for offset in range(first, first + count):
                    slot = lax.rem(lone + offset, shards)
                    term = jnp.dot(
                        acts[copy, slot, at, :], grads[copy][slot], preferred_element_type=jnp.float32
                    )
                    total = term if total is None else total + term
                sums.append(total)
            prior = (sums[0] * sums[0] + sums[1] * sums[1]) * (1.0 / SEQS) + smoothing
            term = prior * weights[copy][at, :].astype(jnp.float32)
            numer = term if numer is None else numer + term
            denom = prior if denom is None else denom + prior
        out_ref[at, :] = (numer / denom).astype(out_ref.dtype)
        return carry

    lax.fori_loop(0, rows // height, row_tile, 0)


def merge_rows(place, slots, own, low, high, grads, weights):
    copies, shards = len(grads), grads[0].shape[0]
    tok, width = grads[0].shape[1:]
    rows = own.shape[1]
    return pl.pallas_call(
        functools.partial(merge_kernel, copies, shards),
        out_shape=jax.ShapeDtypeStruct((rows, width), jnp.bfloat16),
        grid_spec=pltpu.PrefetchScalarGridSpec(
            num_scalar_prefetch=2,
            grid=(width // COL_TILE,),
            in_specs=[pl.BlockSpec(memory_space=pl.ANY)] * (2 * shards - 1)
            + [pl.BlockSpec((shards, tok, COL_TILE), lambda j, *_: (0, 0, j))] * copies
            + [pl.BlockSpec((rows, COL_TILE), lambda j, *_: (0, j))] * copies,
            out_specs=pl.BlockSpec((rows, COL_TILE), lambda j, *_: (0, j)),
            scratch_shapes=[
                pltpu.VMEM((copies, shards, rows, tok), jnp.bfloat16),
                pltpu.SemaphoreType.DMA,
            ],
        ),
        compiler_params=pltpu.CompilerParams(vmem_limit_bytes=56 * 1024 * 1024),
        cost_estimate=pl.CostEstimate(
            flops=2 * copies * shards * tok * rows * width,
            bytes_accessed=2 * copies * (shards * tok * (rows + width) + rows * width) + 2 * rows * width,
            transcendentals=0,
        ),
    )(place, slots, own, *low, *high, *grads, *weights)


def after(value, *others):
    return lax.optimization_barrier((value, *others))[0]


def per_device(activations, out_grads, seq_ids, weights):
    copies = lax.axis_size("mp")
    devices = lax.axis_size("fsdp")
    rows, width = weights.shape[1:]
    blocks = F // width
    spread = devices // blocks
    tok = activations.shape[1]
    share = rows // copies
    part = share // CHUNKS
    piece = share // PIECES
    m = lax.axis_index("mp")
    i = lax.axis_index("fsdp")
    a, h = i // spread, i % spread
    chip, core = m // 2, m % 2

    def to_copy(value, flip):
        return lax.ppermute(value, "mp", [(s, s ^ flip) for s in range(copies)])

    def to_block(value, shift):
        pairs = [(s, (s // spread + shift) % blocks * spread + s % spread) for s in range(devices)]
        return lax.ppermute(value, "fsdp", pairs)

    def to_half(value, shift):
        pairs = [(s, s // spread * spread + (s % spread + shift) % spread) for s in range(devices)]
        return lax.ppermute(value, "fsdp", pairs)

    def along(value, step, direction):
        pairs = [
            (s, s + direction * spread)
            for s in range(devices)
            if 0 <= s // spread + direction < blocks and 0 <= s // spread - direction * (step - 1) < blocks
        ]
        return lax.ppermute(value, "fsdp", pairs)

    def column_block(value, shift):
        return lax.dynamic_slice_in_dim(value, (a + shift) % blocks * width, width, 1)

    def spread_blocks(value):
        return [column_block(value, 0)] + [to_block(column_block(value, k), k) for k in range(1, blocks)]

    def weight_rows(owner, start, count):
        return lax.dynamic_slice_in_dim(weights[0], owner * share + start, count, 0)

    grad_far = to_copy(out_grads[0], 2)
    acts = activations[0].T.reshape(spread, copies // 2, 2, share, tok)
    acts_near = lax.dynamic_index_in_dim(acts, chip, 1, keepdims=False)
    acts_far = to_copy(lax.dynamic_index_in_dim(acts, 1 - chip, 1, keepdims=False), 2)
    near = spread_blocks(out_grads[0])
    grad_near = jnp.stack(near)

    held = jnp.stack([acts_near, acts_far])
    held = after(held, grad_near, grad_far)
    grad_far = after(grad_far, grad_near, held)
    weight_far = []

    def send_weights(k, *others):
        start = k * piece
        both = jnp.stack([weight_rows((1 - chip) * 2 + c, start, piece) for c in range(2)])
        weight_far.append(to_copy(after(both, *others), 2))

    send_weights(0, grad_near, grad_far, held)
    halves = [
        lax.dynamic_index_in_dim(held, (h + d) % spread, 1, keepdims=False) for d in range(spread)
    ]
    halves = [halves[0]] + [to_half(halves[d], d) for d in range(1, spread)]
    held = jnp.stack(halves, 1)
    acts_mine = lax.dynamic_index_in_dim(held, core, 2, keepdims=False)
    acts_mate = to_copy(lax.dynamic_index_in_dim(held, 1 - core, 2, keepdims=False), 1)
    shard = jnp.stack([acts_mine, acts_mate], 1).reshape(copies * spread, share, tok)
    flags = jnp.where(jnp.arange(copies) == m, seq_ids[0, 0], 0)
    flags = after(flags, grad_near)
    flags = flags + to_copy(flags, 2)
    grad_far = jnp.stack(spread_blocks(grad_far))

    stage = (shard, grad_far, weight_far[0], flags)
    shards = [shard[:, k * part:(k + 1) * part] for k in range(CHUNKS)]
    low = [[] for _ in range(CHUNKS)]
    high = [[] for _ in range(CHUNKS)]
    grads = [None] * copies

    def step(k, *others):
        n = len(low[k]) + 1
        right, left = (low[k][-1], high[k][-1]) if n > 1 else (shards[k], shards[k])
        low[k].append(along(after(right, *others), n, 1))
        high[k].append(along(after(left, *others), n, -1))

    def over_halves(value):
        return jnp.concatenate([value] + [to_half(value, d) for d in range(1, spread)], axis=1)

    step(0, *stage)
    step(0)
    send_weights(1, *stage)
    grads[0] = over_halves(after(grad_near, *stage))
    mate_rows = to_copy(after(weight_rows(chip * 2 + 1 - core, 0, share), *stage), 1)
    flags = flags + to_copy(after(flags, *stage), 1)
    stage = (low[0][-1], high[0][-1], weight_far[1], grads[0], mate_rows, flags)
    step(0, *stage)
    step(1, *stage)
    send_weights(2, *stage)
    grads[2] = over_halves(after(grad_far, *stage))
    grads[1] = to_copy(after(grads[0], *stage), 1)
    ends = [(s, s - spread) for s in range(spread, 2 * spread)]
    ends += [(s, s + spread) for s in range(devices - 2 * spread, devices - spread)]
    outer = lax.ppermute(after(flags, *stage), "fsdp", ends)
    flags = jnp.where((a == 0) | (a == blocks - 1), outer, flags)
    stage = (low[0][-1], high[0][-1], low[1][-1], high[1][-1], weight_far[2], grads[1], grads[2], flags)
    step(1, *stage)
    step(1)
    send_weights(3, *stage)
    grads[3] = to_copy(after(grads[2], *stage), 1)

    alone = jnp.where(flags == 1, 0, blocks - 1)[m ^ jnp.arange(copies)]
    slots = ((a - alone) % blocks).astype(jnp.int32)
    place = a.astype(jnp.int32)[None]

    merged = None
    count = PIECES // CHUNKS
    for chunk in range(CHUNKS):
        far = jnp.concatenate(weight_far[chunk * count:(chunk + 1) * count], axis=1)
        mine = lax.dynamic_index_in_dim(far, core, 0, keepdims=False)
        mate = to_copy(lax.dynamic_index_in_dim(far, 1 - core, 0, keepdims=False), 1)
        held = [weight_rows(m, chunk * part, part), mate_rows[chunk * part:(chunk + 1) * part], mine, mate]
        mine = merge_rows(place, slots, shards[chunk], low[chunk], high[chunk], grads, held)
        far = to_copy(mine, 2)
        if merged is None:
            merged = jnp.zeros((rows, width), jnp.bfloat16)
        for flip, value in ((0, mine), (1, to_copy(mine, 1)), (2, far), (3, to_copy(far, 1))):
            merged = lax.dynamic_update_slice_in_dim(merged, value, (m ^ flip) * share + chunk * part, 0)
    return merged


def solution(mesh):
    placed = (P("mp", "fsdp", None), P("mp", "fsdp", None), P("mp", "fsdp"), P("mp", "fsdp", None))
    return jax.shard_map(
        per_device, mesh=mesh, in_specs=placed, out_specs=P("fsdp", None), check_vma=False
    )
```

```python
import functools

import jax
import jax.numpy as jnp
from jax import lax
from jax.experimental import pallas as pl
from jax.experimental.pallas import tpu as pltpu
from jax.sharding import PartitionSpec as P

F = 7168
SEQS = 2
CHUNKS = (4, 4, 5, 3)
FLAG_ROWS = 16
COL_TILE = 256

smoothing = 0.05


def merge_kernel(copies, shards, starts, place_ref, slot_ref, *refs):
    count = 2 * shards - 1
    sources, refs = refs[:count], refs[count:]
    grads = refs[:copies]
    weights = refs[copies:2 * copies]
    out_ref, acts, sem = refs[2 * copies:]
    rows = acts.shape[2]
    tok = sources[0].shape[2]
    spread = sources[0].shape[0] // copies
    a = place_ref[0]

    def fetch(n, slot):
        for copy in range(copies):
            for part in range(spread):
                pltpu.make_async_copy(
                    sources[n].at[copy * spread + part, pl.ds(starts[n], rows), :],
                    acts.at[copy, slot, :, pl.ds(part * tok, tok)],
                    sem,
                ).start()

    @pl.when(pl.program_id(0) == 0)
    def _():
        fetch(0, 0)
        for slot in range(1, shards):
            @pl.when(a >= slot)
            def _(slot=slot):
                fetch(slot, slot)

            @pl.when(a < slot)
            def _(slot=slot):
                fetch(2 * shards - 1 - slot, slot)
        pltpu.make_async_copy(acts, acts, sem).wait()

    numer = denom = None
    for copy in range(copies):
        sums = []
        lone = slot_ref[copy]
        for first, count in ((0, 1), (1, shards - 1)):
            total = None
            for offset in range(first, first + count):
                slot = lax.rem(lone + offset, shards)
                term = jnp.dot(acts[copy, slot], grads[copy][slot], preferred_element_type=jnp.float32)
                total = term if total is None else total + term
            sums.append(total)
        prior = (sums[0] * sums[0] + sums[1] * sums[1]) * (1.0 / SEQS) + smoothing
        term = prior * weights[copy][...].astype(jnp.float32)
        numer = term if numer is None else numer + term
        denom = prior if denom is None else denom + prior
    out_ref[...] = (numer / denom).astype(out_ref.dtype)


def merge_rows(place, slots, sources, starts, grads, weights):
    copies, shards = len(grads), grads[0].shape[0]
    tok, width = grads[0].shape[1:]
    rows = weights[0].shape[0]
    return pl.pallas_call(
        functools.partial(merge_kernel, copies, shards, starts),
        out_shape=jax.ShapeDtypeStruct((rows, width), jnp.bfloat16),
        grid_spec=pltpu.PrefetchScalarGridSpec(
            num_scalar_prefetch=2,
            grid=(width // COL_TILE,),
            in_specs=[pl.BlockSpec(memory_space=pl.ANY)] * len(sources)
            + [pl.BlockSpec((shards, tok, COL_TILE), lambda j, *_: (0, 0, j))] * copies
            + [pl.BlockSpec((rows, COL_TILE), lambda j, *_: (0, j))] * copies,
            out_specs=pl.BlockSpec((rows, COL_TILE), lambda j, *_: (0, j)),
            scratch_shapes=[
                pltpu.VMEM((copies, shards, rows, tok), jnp.bfloat16),
                pltpu.SemaphoreType.DMA,
            ],
        ),
        compiler_params=pltpu.CompilerParams(vmem_limit_bytes=56 * 1024 * 1024),
        cost_estimate=pl.CostEstimate(
            flops=2 * copies * shards * tok * rows * width,
            bytes_accessed=2 * copies * (shards * tok * (rows + width) + rows * width) + 2 * rows * width,
            transcendentals=0,
        ),
    )(place, slots, *sources, *grads, *weights)


def place_kernel(count, where_ref, *refs):
    pieces, (out_ref, sems) = refs[:count], refs[-2:]
    moves = [
        pltpu.make_async_copy(
            piece,
            out_ref.at[pl.ds(pl.multiple_of(where_ref[n], 16), piece.shape[0]), :],
            sems.at[n],
        )
        for n, piece in enumerate(pieces)
    ]
    for move in moves:
        move.start()
    for move in moves:
        move.wait()


def place_rows(total, pieces, where, whole):
    count = len(pieces)
    shape = jax.ShapeDtypeStruct((total, pieces[0].shape[1]), pieces[0].dtype)
    more = [] if whole is None else [whole]
    return pl.pallas_call(
        functools.partial(place_kernel, count),
        out_shape=shape,
        grid_spec=pltpu.PrefetchScalarGridSpec(
            num_scalar_prefetch=1,
            grid=(1,),
            in_specs=[pl.BlockSpec(memory_space=pl.ANY)] * (count + len(more)),
            out_specs=pl.BlockSpec(memory_space=pl.ANY),
            scratch_shapes=[pltpu.SemaphoreType.DMA((count,))],
        ),
        input_output_aliases={1 + count: 0} if more else {},
        cost_estimate=pl.CostEstimate(
            flops=0, bytes_accessed=4 * sum(p.size for p in pieces), transcendentals=0
        ),
    )(jnp.stack(where).astype(jnp.int32), *pieces, *more)


def after(value, *others):
    return lax.optimization_barrier((value, *others))[0]


def per_device(activations, out_grads, seq_ids, weights):
    copies = lax.axis_size("mp")
    devices = lax.axis_size("fsdp")
    rows, width = weights.shape[1:]
    blocks = F // width
    spread = devices // blocks
    tok = activations.shape[1]
    share = rows // copies
    sizes = [share * n // sum(CHUNKS) for n in CHUNKS]
    starts = [sum(sizes[:k]) for k in range(len(sizes))]
    m = lax.axis_index("mp")
    i = lax.axis_index("fsdp")
    a, h = i // spread, i % spread
    chip, core = m // 2, m % 2

    def to_copy(value, flip):
        return lax.ppermute(value, "mp", [(s, s ^ flip) for s in range(copies)])

    def to_block(value, shift):
        pairs = [(s, (s // spread + shift) % blocks * spread + s % spread) for s in range(devices)]
        return lax.ppermute(value, "fsdp", pairs)

    def to_half(value, shift):
        pairs = [(s, s // spread * spread + (s % spread + shift) % spread) for s in range(devices)]
        return lax.ppermute(value, "fsdp", pairs)

    def along(value, step, direction):
        pairs = [
            (s, s + direction * spread)
            for s in range(devices)
            if 0 <= s // spread + direction < blocks and 0 <= s // spread - direction * (step - 1) < blocks
        ]
        return lax.ppermute(value, "fsdp", pairs)

    def spread_blocks(value):
        cut = [lax.dynamic_slice_in_dim(value, (a + k) % blocks * width, width, 1) for k in range(blocks)]
        return jnp.stack([cut[0]] + [to_block(cut[k], k) for k in range(1, blocks)])

    def over_halves(value):
        return jnp.concatenate([value] + [to_half(value, d) for d in range(1, spread)], axis=1)

    def weight_rows(owner, k):
        return lax.dynamic_slice_in_dim(weights[0], owner * share + starts[k], sizes[k], 0)

    weight_far, weight_mate = [None] * len(sizes), [None] * len(sizes)

    def send_weights(k, *others):
        both = jnp.stack([weight_rows((1 - chip) * 2 + c, k) for c in range(2)])
        weight_far[k] = to_copy(after(both, *others), 2)

    grad_far = to_copy(out_grads[0], 2)
    grad_near = spread_blocks(out_grads[0])

    acts = activations[0].T.reshape(spread, copies // 2, 2, share, tok)
    named = jnp.broadcast_to(seq_ids[0].astype(acts.dtype), acts.shape[:3] + (FLAG_ROWS, tok))
    acts = jnp.concatenate([acts, named], axis=3)
    acts_near = lax.dynamic_index_in_dim(acts, chip, 1, keepdims=False)
    acts_far = lax.dynamic_index_in_dim(acts, 1 - chip, 1, keepdims=False)
    acts_far = to_copy(after(acts_far, grad_far), 2)
    grad_far = spread_blocks(after(grad_far, grad_near))
    send_weights(3, acts_far)
    held = jnp.stack([acts_near, acts_far])
    halves = [lax.dynamic_index_in_dim(held, (h + d) % spread, 1, keepdims=False) for d in range(spread)]
    halves = [halves[0]] + [to_half(halves[d], d) for d in range(1, spread)]
    held = jnp.stack(halves, 1)
    acts_mine = lax.dynamic_index_in_dim(held, core, 2, keepdims=False)
    acts_mate = to_copy(lax.dynamic_index_in_dim(held, 1 - core, 2, keepdims=False), 1)
    own = jnp.stack([acts_mine, acts_mate], 1).reshape(copies * spread, share + FLAG_ROWS, tok)

    grads = [None] * copies
    stage = (own, grad_far, weight_far[3])
    low, high = [along(after(own, *stage), 1, 1)], [along(after(own, *stage), 1, -1)]
    send_weights(0, *stage)
    grads[0] = over_halves(after(grad_near, *stage))
    mate_rows = lax.dynamic_slice_in_dim(weights[0], (chip * 2 + 1 - core) * share, share, 0)
    mate_rows = to_copy(after(mate_rows, *stage), 1)

    stage = (low[0], high[0], weight_far[0], grads[0], mate_rows)
    low.append(along(after(low[0], *stage), 2, 1))
    high.append(along(after(high[0], *stage), 2, -1))
    send_weights(1, *stage)
    grads[2] = over_halves(after(grad_far, *stage))
    grads[1] = to_copy(after(grads[0], *stage), 1)
    named = jnp.where(a == 0, high[0][:, share, 0], jnp.where(a == blocks - 1, low[0][:, share, 0], own[:, share, 0]))
    alone = jnp.where(named[::spread] > 0.5, 0, blocks - 1)
    slots = ((a - alone) % blocks).astype(jnp.int32)
    place = a.astype(jnp.int32)[None]

    stage = (low[1], high[1], weight_far[1], grads[1], grads[2])
    grads[3] = to_copy(after(grads[2], *stage), 1)
    send_weights(2, *stage)
    half = starts[2]
    low_last, high_last = [], []
    for first, count in ((0, half), (half, share - half)):
        cut = (slice(None), slice(first, first + count))
        low_last.append(along(after(low[1][cut], *stage), 3, 1))
        high_last.append(along(after(high[1][cut], *stage), 3, -1))

    wholes = [None]
    for k in range(len(sizes)):
        mine = lax.dynamic_index_in_dim(weight_far[k], core, 0, keepdims=False)
        mate = to_copy(lax.dynamic_index_in_dim(weight_far[k], 1 - core, 0, keepdims=False), 1)
        held = [weight_rows(m, k), mate_rows[starts[k]:starts[k] + sizes[k]], mine, mate]
        part = k // 2
        sources = [own, low[0], low[1], low_last[part], high[0], high[1], high_last[part]]
        begin = [starts[k]] * 7
        begin[3] = begin[6] = starts[k] - part * half
        mine = merge_rows(place, slots, sources, begin, grads, held)
        place = after(place, mine)
        if k == len(sizes) - 1:
            mine = after(mine, wholes[-2])
        far = to_copy(mine, 2)
        pieces = [mine, to_copy(mine, 1), far, to_copy(far, 1)]
        where = [(m ^ flip) * share + starts[k] for flip in range(copies)]
        wholes.append(place_rows(rows, pieces, where, wholes[-1]))
    return wholes[-1]


def solution(mesh):
    placed = (P("mp", "fsdp", None), P("mp", "fsdp", None), P("mp", "fsdp"), P("mp", "fsdp", None))
    return jax.shard_map(
        per_device, mesh=mesh, in_specs=placed, out_specs=P("fsdp", None), check_vma=False
    )
```

```python
import functools

import jax
import jax.numpy as jnp
from jax import lax
from jax.experimental import pallas as pl
from jax.experimental.pallas import tpu as pltpu
from jax.sharding import PartitionSpec as P

F = 7168
SEQS = 2
CHUNKS = (16, 20, 20, 8)
FLAG_ROWS = 16
COL_TILE = 256

smoothing = 0.05


def merge_kernel(copies, shards, starts, sizes, place_ref, slot_ref, *refs):
    count = 2 * shards - 1
    sources, refs = refs[:count], refs[count:]
    grads = refs[:copies]
    weights, (out_ref, acts, sem) = refs[copies:-3], refs[-3:]
    rows = acts.shape[2]
    tok = sources[0].shape[2]
    spread = sources[0].shape[0] // copies
    a, m, h = place_ref[0], place_ref[1], place_ref[2]

    def fetch(n, slot):
        for copy in range(copies):
            for part in range(spread):
                pltpu.make_async_copy(
                    sources[n].at[
                        lax.bitwise_xor(m, copy) * spread + lax.rem(h + spread - part, spread),
                        pl.ds(starts[n], rows),
                        :,
                    ],
                    acts.at[copy, slot, :, pl.ds(part * tok, tok)],
                    sem,
                ).start()

    @pl.when(pl.program_id(0) == 0)
    def _():
        fetch(0, 0)
        for slot in range(1, shards):
            @pl.when(a >= slot)
            def _(slot=slot):
                fetch(slot, slot)

            @pl.when(a < slot)
            def _(slot=slot):
                fetch(2 * shards - 1 - slot, slot)
        pltpu.make_async_copy(acts, acts, sem).wait()

    first = 0
    for piece, size in enumerate(sizes):
        at = slice(first, first + size)
        numer = denom = None
        for copy in range(copies):
            sums = []
            lone = slot_ref[copy]
            for offset, count in ((0, 1), (1, shards - 1)):
                total = None
                for n in range(offset, offset + count):
                    slot = lax.rem(lone + n, shards)
                    term = jnp.dot(
                        acts[copy, slot, at, :], grads[copy][slot], preferred_element_type=jnp.float32
                    )
                    total = term if total is None else total + term
                sums.append(total)
            prior = (sums[0] * sums[0] + sums[1] * sums[1]) * (1.0 / SEQS) + smoothing
            term = prior * weights[piece * copies + copy][...].astype(jnp.float32)
            numer = term if numer is None else numer + term
            denom = prior if denom is None else denom + prior
        out_ref[at, :] = (numer / denom).astype(out_ref.dtype)
        first += size


def merge_rows(place, slots, sources, starts, grads, weights):
    copies, shards = len(grads), grads[0].shape[0]
    tok, width = grads[0].shape[1:]
    sizes = [piece.shape[0] for piece in weights[::copies]]
    rows = sum(sizes)
    return pl.pallas_call(
        functools.partial(merge_kernel, copies, shards, starts, sizes),
        out_shape=jax.ShapeDtypeStruct((rows, width), jnp.bfloat16),
        grid_spec=pltpu.PrefetchScalarGridSpec(
            num_scalar_prefetch=2,
            grid=(width // COL_TILE,),
            in_specs=[pl.BlockSpec(memory_space=pl.ANY)] * len(sources)
            + [pl.BlockSpec((shards, tok, COL_TILE), lambda j, *_: (0, 0, j))] * copies
            + [pl.BlockSpec((piece.shape[0], COL_TILE), lambda j, *_: (0, j)) for piece in weights],
            out_specs=pl.BlockSpec((rows, COL_TILE), lambda j, *_: (0, j)),
            scratch_shapes=[
                pltpu.VMEM((copies, shards, rows, tok), jnp.bfloat16),
                pltpu.SemaphoreType.DMA,
            ],
        ),
        compiler_params=pltpu.CompilerParams(vmem_limit_bytes=56 * 1024 * 1024),
        cost_estimate=pl.CostEstimate(
            flops=2 * copies * shards * tok * rows * width, bytes_accessed=2 * copies * shards * tok * width, transcendentals=0
        ),
    )(place, slots, *sources, *grads, *weights)


def place_kernel(count, where_ref, *refs):
    pieces, (out_ref, sems) = refs[:count], refs[-2:]
    moves = [
        pltpu.make_async_copy(
            piece,
            out_ref.at[pl.ds(pl.multiple_of(where_ref[n], 16), piece.shape[0]), :],
            sems.at[n],
        )
        for n, piece in enumerate(pieces)
    ]
    for move in moves:
        move.start()
    for move in moves:
        move.wait()


def place_rows(total, pieces, where, whole):
    count = len(pieces)
    shape = jax.ShapeDtypeStruct((total, pieces[0].shape[1]), pieces[0].dtype)
    more = [] if whole is None else [whole]
    return pl.pallas_call(
        functools.partial(place_kernel, count),
        out_shape=shape,
        grid_spec=pltpu.PrefetchScalarGridSpec(
            num_scalar_prefetch=1,
            grid=(1,),
            in_specs=[pl.BlockSpec(piece.shape, lambda *_: (0, 0)) for piece in pieces]
            + [pl.BlockSpec(memory_space=pl.ANY)] * len(more),
            out_specs=pl.BlockSpec(memory_space=pl.ANY),
            scratch_shapes=[pltpu.SemaphoreType.DMA((count,))],
        ),
        input_output_aliases={1 + count: 0} if more else {},
        compiler_params=pltpu.CompilerParams(vmem_limit_bytes=32 * 1024 * 1024),
        cost_estimate=pl.CostEstimate(
            flops=0, bytes_accessed=4 * sum(p.size for p in pieces), transcendentals=0
        ),
    )(jnp.stack(where).astype(jnp.int32), *pieces, *more)


def after(value, *others):
    return lax.optimization_barrier((value, *others))[0]


def per_device(activations, out_grads, seq_ids, weights):
    copies = lax.axis_size("mp")
    devices = lax.axis_size("fsdp")
    rows, width = weights.shape[1:]
    blocks = F // width
    spread = devices // blocks
    tok = activations.shape[1]
    share = rows // copies
    sizes = [share * n // sum(CHUNKS) for n in CHUNKS]
    starts = [sum(sizes[:k]) for k in range(len(sizes))]
    m = lax.axis_index("mp")
    i = lax.axis_index("fsdp")
    a, h = i // spread, i % spread
    chip, core = m // 2, m % 2

    def to_copy(value, flip):
        return lax.ppermute(value, "mp", [(s, s ^ flip) for s in range(copies)])

    def to_block(value, shift):
        pairs = [(s, (s // spread + shift) % blocks * spread + s % spread) for s in range(devices)]
        return lax.ppermute(value, "fsdp", pairs)

    def to_half(value, shift):
        pairs = [(s, s // spread * spread + (s % spread + shift) % spread) for s in range(devices)]
        return lax.ppermute(value, "fsdp", pairs)

    def along(value, step, direction):
        pairs = [
            (s, s + direction * spread)
            for s in range(devices)
            if 0 <= s // spread + direction < blocks and 0 <= s // spread - direction * (step - 1) < blocks
        ]
        return lax.ppermute(value, "fsdp", pairs)

    def spread_blocks(value):
        cut = [lax.dynamic_slice_in_dim(value, (a + k) % blocks * width, width, 1) for k in range(blocks)]
        return jnp.stack([cut[0]] + [to_block(cut[k], k) for k in range(1, blocks)])

    def over_halves(value):
        return jnp.concatenate([value] + [to_half(value, d) for d in range(1, spread)], axis=1)

    def weight_rows(owner, k):
        return lax.dynamic_slice_in_dim(weights[0], owner * share + starts[k], sizes[k], 0)

    def mate(value, *others):
        return to_copy(after(value, *others), 1)

    grad_far = to_copy(out_grads[0], 2)
    grad_near = spread_blocks(out_grads[0])
    acts = activations[0].T.reshape(spread, copies, share, tok).transpose(1, 0, 2, 3)
    named = jnp.broadcast_to(seq_ids[0].astype(acts.dtype), acts.shape[:2] + (FLAG_ROWS, tok))
    acts = jnp.concatenate([acts, named], axis=2).reshape(copies * spread, share + FLAG_ROWS, tok)
    planes = [
        [c * devices + block * spread + s for c in range(copies) for s in range(spread)] for block in range(blocks)
    ]
    own = lax.all_to_all(acts, ("mp", "fsdp"), 0, 0, axis_index_groups=planes, tiled=True)
    leaving = [jnp.stack([weight_rows((1 - chip) * 2 + c, k) for c in range(2)]) for k in range(len(sizes))]
    mate_rows = lax.dynamic_slice_in_dim(weights[0], (chip * 2 + 1 - core) * share, share, 0)

    weight_far = [None] * len(sizes)
    weight_mate = [None] * len(sizes)

    def send_weights(k, *others):
        weight_far[k] = to_copy(after(leaving[k], *others), 2)

    def cores(k, *others):
        weight_mate[k] = mate(lax.dynamic_index_in_dim(weight_far[k], 1 - core, 0, keepdims=False), *others)

    grads = [None] * copies
    stage = (own, grad_near, mate_rows, *leaving)
    low, high = [along(after(own, *stage), 1, 1)], [along(after(own, *stage), 1, -1)]
    send_weights(0, *stage, grad_far)
    grads[0] = over_halves(after(grad_near, *stage))

    stage = (low[0], high[0], grad_far, grads[0], weight_far[0])
    grad_far = spread_blocks(after(grad_far, *stage))
    send_weights(1, *stage)
    grads[1] = mate(grads[0], *stage)
    cores(0, *stage, grads[1])

    stage = (grad_far, grads[1], weight_far[1], weight_mate[0])
    low.append(along(after(low[0], *stage), 2, 1))
    high.append(along(after(high[0], *stage), 2, -1))
    send_weights(2, *stage)
    grads[2] = over_halves(after(grad_far, *stage))
    mate_rows = mate(mate_rows, *stage)
    cores(1, *stage, mate_rows)
    named = jnp.where(a == 0, high[0][:, share, 0], jnp.where(a == blocks - 1, low[0][:, share, 0], own[:, share, 0]))
    alone = jnp.where(named[::spread] > 0.5, 0, blocks - 1)[m ^ jnp.arange(copies)]
    slots = ((a - alone) % blocks).astype(jnp.int32)
    place = jnp.stack([a, m, h]).astype(jnp.int32)

    stage = (low[1], high[1], weight_far[2], grads[1], grads[2], weight_mate[1], slots)
    half = starts[2]
    grads[3] = mate(grads[2], *stage)
    low_last = [along(after(low[1], *stage)[:, :half], 3, 1)]
    high_last = [along(after(high[1], *stage)[:, :half], 3, -1)]
    low_last.append(along(after(low[1], *stage)[:, half:share], 3, 1))
    high_last.append(along(after(high[1], *stage)[:, half:share], 3, -1))
    cores(2, *stage, grads[3])
    send_weights(3, *stage)
    cores(3, low_last[0], high_last[0])

    whole = None
    for part in range(2):
        held = []
        for k in (2 * part, 2 * part + 1):
            mine = lax.dynamic_index_in_dim(weight_far[k], core, 0, keepdims=False)
            held += [weight_rows(m, k), mate_rows[starts[k]:starts[k] + sizes[k]], mine, weight_mate[k]]
        if part == 0:
            place = after(place, weight_far[3], weight_mate[2])
        sources = [own, low[0], low[1], low_last[part], high[0], high[1], high_last[part]]
        begin = [part * half] * len(sources)
        begin[3] = begin[6] = 0
        mine = merge_rows(place, slots, sources, begin, grads, held)
        if part == 0:
            place = after(place, mine)
        far = to_copy(mine, 2)
        last = far if whole is None else after(far, whole)
        pieces = [mine, to_copy(mine, 1), far, to_copy(last, 1)]
        where = [(m ^ flip) * share + part * half for flip in range(copies)]
        whole = place_rows(rows, pieces, where, whole)
    return whole


def solution(mesh):
    placed = (P("mp", "fsdp", None), P("mp", "fsdp", None), P("mp", "fsdp"), P("mp", "fsdp", None))
    return jax.shard_map(
        per_device, mesh=mesh, in_specs=placed, out_specs=P("fsdp", None), check_vma=False
    )
```

```python
import functools

import jax
import jax.numpy as jnp
from jax import lax
from jax.experimental import pallas as pl
from jax.experimental.pallas import tpu as pltpu
from jax.sharding import PartitionSpec as P

F = 7168
SEQS = 2
CHUNKS = (16, 20, 20, 8)
FLAG_ROWS = 16
COL_TILE = 256

smoothing = 0.05


def merge_kernel(copies, shards, starts, sizes, place_ref, slot_ref, *refs):
    count = 2 * shards - 1
    sources, refs = refs[:count], refs[count:]
    grads = refs[:copies]
    weights, (out_ref, acts, sem) = refs[copies:-3], refs[-3:]
    rows = acts.shape[2]
    tok = sources[0].shape[2]
    spread = sources[0].shape[0] // copies
    a, m, h = place_ref[0], place_ref[1], place_ref[2]

    def fetch(n, slot):
        for copy in range(copies):
            for part in range(spread):
                pltpu.make_async_copy(
                    sources[n].at[
                        lax.bitwise_xor(m, copy) * spread + lax.rem(h + spread - part, spread),
                        pl.ds(starts[n], rows),
                        :,
                    ],
                    acts.at[copy, slot, :, pl.ds(part * tok, tok)],
                    sem,
                ).start()

    @pl.when(pl.program_id(0) == 0)
    def _():
        fetch(0, 0)
        for slot in range(1, shards):
            @pl.when(a >= slot)
            def _(slot=slot):
                fetch(slot, slot)

            @pl.when(a < slot)
            def _(slot=slot):
                fetch(2 * shards - 1 - slot, slot)
        pltpu.make_async_copy(acts, acts, sem).wait()

    first = 0
    for piece, size in enumerate(sizes):
        at = slice(first, first + size)
        numer = denom = None
        for copy in range(copies):
            sums = []
            lone = slot_ref[copy]
            for offset, count in ((0, 1), (1, shards - 1)):
                total = None
                for n in range(offset, offset + count):
                    slot = lax.rem(lone + n, shards)
                    term = jnp.dot(
                        acts[copy, slot, at, :], grads[copy][slot], preferred_element_type=jnp.float32
                    )
                    total = term if total is None else total + term
                sums.append(total)
            prior = (sums[0] * sums[0] + sums[1] * sums[1]) * (1.0 / SEQS) + smoothing
            term = prior * weights[piece * copies + copy][...].astype(jnp.float32)
            numer = term if numer is None else numer + term
            denom = prior if denom is None else denom + prior
        out_ref[at, :] = (numer / denom).astype(out_ref.dtype)
        first += size


def merge_rows(place, slots, sources, starts, grads, weights):
    copies, shards = len(grads), grads[0].shape[0]
    tok, width = grads[0].shape[1:]
    sizes = [piece.shape[0] for piece in weights[::copies]]
    rows = sum(sizes)
    return pl.pallas_call(
        functools.partial(merge_kernel, copies, shards, starts, sizes),
        out_shape=jax.ShapeDtypeStruct((rows, width), jnp.bfloat16),
        grid_spec=pltpu.PrefetchScalarGridSpec(
            num_scalar_prefetch=2,
            grid=(width // COL_TILE,),
            in_specs=[pl.BlockSpec(memory_space=pl.ANY)] * len(sources)
            + [pl.BlockSpec((shards, tok, COL_TILE), lambda j, *_: (0, 0, j))] * copies
            + [pl.BlockSpec((piece.shape[0], COL_TILE), lambda j, *_: (0, j)) for piece in weights],
            out_specs=pl.BlockSpec((rows, COL_TILE), lambda j, *_: (0, j)),
            scratch_shapes=[
                pltpu.VMEM((copies, shards, rows, tok), jnp.bfloat16),
                pltpu.SemaphoreType.DMA,
            ],
        ),
        compiler_params=pltpu.CompilerParams(vmem_limit_bytes=56 * 1024 * 1024),
        cost_estimate=pl.CostEstimate(
            flops=2 * copies * shards * tok * rows * width, bytes_accessed=2 * copies * shards * tok * width, transcendentals=0
        ),
    )(place, slots, *sources, *grads, *weights)


def place_kernel(count, where_ref, *refs):
    pieces, (out_ref, sems) = refs[:count], refs[-2:]
    moves = [
        pltpu.make_async_copy(
            piece,
            out_ref.at[pl.ds(pl.multiple_of(where_ref[n], 16), piece.shape[0]), :],
            sems.at[n],
        )
        for n, piece in enumerate(pieces)
    ]
    for move in moves:
        move.start()
    for move in moves:
        move.wait()


def place_rows(total, pieces, where, whole):
    count = len(pieces)
    shape = jax.ShapeDtypeStruct((total, pieces[0].shape[1]), pieces[0].dtype)
    more = [] if whole is None else [whole]
    return pl.pallas_call(
        functools.partial(place_kernel, count),
        out_shape=shape,
        grid_spec=pltpu.PrefetchScalarGridSpec(
            num_scalar_prefetch=1,
            grid=(1,),
            in_specs=[pl.BlockSpec(piece.shape, lambda *_: (0, 0)) for piece in pieces]
            + [pl.BlockSpec(memory_space=pl.ANY)] * len(more),
            out_specs=pl.BlockSpec(memory_space=pl.ANY),
            scratch_shapes=[pltpu.SemaphoreType.DMA((count,))],
        ),
        input_output_aliases={1 + count: 0} if more else {},
        compiler_params=pltpu.CompilerParams(vmem_limit_bytes=32 * 1024 * 1024),
        cost_estimate=pl.CostEstimate(
            flops=0, bytes_accessed=4 * sum(p.size for p in pieces), transcendentals=0
        ),
    )(jnp.stack(where).astype(jnp.int32), *pieces, *more)


def after(value, *others):
    return lax.optimization_barrier((value, *others))[0]


def per_device(activations, out_grads, seq_ids, weights):
    copies = lax.axis_size("mp")
    devices = lax.axis_size("fsdp")
    rows, width = weights.shape[1:]
    blocks = F // width
    spread = devices // blocks
    tok = activations.shape[1]
    share = rows // copies
    sizes = [share * n // sum(CHUNKS) for n in CHUNKS]
    starts = [sum(sizes[:k]) for k in range(len(sizes))]
    m = lax.axis_index("mp")
    i = lax.axis_index("fsdp")
    a, h = i // spread, i % spread
    chip, core = m // 2, m % 2

    def to_copy(value, flip):
        return lax.ppermute(value, "mp", [(s, s ^ flip) for s in range(copies)])

    def to_block(value, shift):
        pairs = [(s, (s // spread + shift) % blocks * spread + s % spread) for s in range(devices)]
        return lax.ppermute(value, "fsdp", pairs)

    def to_half(value, shift):
        pairs = [(s, s // spread * spread + (s % spread + shift) % spread) for s in range(devices)]
        return lax.ppermute(value, "fsdp", pairs)

    def along(value, step, direction):
        pairs = [
            (s, s + direction * spread)
            for s in range(devices)
            if 0 <= s // spread + direction < blocks and 0 <= s // spread - direction * (step - 1) < blocks
        ]
        return lax.ppermute(value, "fsdp", pairs)

    def cut_blocks(value):
        return [lax.dynamic_slice_in_dim(value, (a + k) % blocks * width, width, 1) for k in range(blocks)]

    def spread_blocks(cut):
        return jnp.stack([cut[0]] + [to_block(cut[k], k) for k in range(1, blocks)])

    def over_halves(value):
        return jnp.concatenate([value] + [to_half(value, d) for d in range(1, spread)], axis=1)

    def weight_rows(owner, k):
        return lax.dynamic_slice_in_dim(weights[0], owner * share + starts[k], sizes[k], 0)

    def mate(value, *others):
        return to_copy(after(value, *others), 1)

    grad_far = to_copy(out_grads[0], 2)
    cut = cut_blocks(out_grads[0])
    grad_near = spread_blocks(cut)
    acts = after(activations[0], *cut).T.reshape(spread, copies, share, tok).transpose(1, 0, 2, 3)
    named = jnp.broadcast_to(seq_ids[0].astype(acts.dtype), acts.shape[:2] + (FLAG_ROWS, tok))
    acts = jnp.concatenate([acts, named], axis=2).reshape(copies * spread, share + FLAG_ROWS, tok)
    planes = [
        [c * devices + block * spread + s for c in range(copies) for s in range(spread)] for block in range(blocks)
    ]
    own = lax.all_to_all(acts, ("mp", "fsdp"), 0, 0, axis_index_groups=planes, tiled=True)
    leaving = [jnp.stack([weight_rows((1 - chip) * 2 + c, k) for c in range(2)]) for k in range(len(sizes))]
    mate_rows = lax.dynamic_slice_in_dim(weights[0], (chip * 2 + 1 - core) * share, share, 0)
    mate_rows = mate(mate_rows, *cut)

    weight_far = [None] * len(sizes)
    weight_mate = [None] * len(sizes)

    def send_weights(k, *others):
        weight_far[k] = to_copy(after(leaving[k], *others), 2)

    def cores(k, *others):
        weight_mate[k] = mate(lax.dynamic_index_in_dim(weight_far[k], 1 - core, 0, keepdims=False), *others)

    grads = [None] * copies
    stage = (own, grad_near, mate_rows, *leaving)
    early = stage
    low, high = [along(after(own, *stage), 1, 1)], [along(after(own, *stage), 1, -1)]
    send_weights(0, *stage)
    grads[0] = over_halves(after(grad_near, *stage))

    send_weights(1, *early)
    cut = cut_blocks(grad_far)
    stage = (low[0], high[0], grads[0], weight_far[0], *cut)
    early = stage
    grad_far = spread_blocks([after(block, *stage) for block in cut])
    grads[1] = mate(grads[0], *stage)

    stage = (grad_far, grads[1], weight_far[1])
    low.append(along(after(low[0], *stage), 2, 1))
    high.append(along(after(high[0], *stage), 2, -1))
    send_weights(2, *early)
    early = stage
    grads[2] = over_halves(after(grad_far, *stage))
    cores(0, *stage)
    cores(1, weight_mate[0])
    named = jnp.where(a == 0, high[0][:, share, 0], jnp.where(a == blocks - 1, low[0][:, share, 0], own[:, share, 0]))
    alone = jnp.where(named[::spread] > 0.5, 0, blocks - 1)[m ^ jnp.arange(copies)]
    slots = ((a - alone) % blocks).astype(jnp.int32)
    place = jnp.stack([a, m, h]).astype(jnp.int32)

    stage = (low[1], high[1], weight_far[2], grads[1], grads[2], weight_mate[1], slots)
    half = starts[2]
    grads[3] = mate(grads[2], *stage)
    low_last = [along(after(low[1], *stage)[:, :half], 3, 1)]
    high_last = [along(after(high[1], *stage)[:, :half], 3, -1)]
    low_last.append(along(after(low[1], *stage)[:, half:share], 3, 1))
    high_last.append(along(after(high[1], *stage)[:, half:share], 3, -1))
    cores(2, *stage, grads[3])
    send_weights(3, *early)
    cores(3, low_last[0], high_last[0])

    merged = []
    for part in range(2):
        held = []
        for k in (2 * part, 2 * part + 1):
            mine = lax.dynamic_index_in_dim(weight_far[k], core, 0, keepdims=False)
            held += [weight_rows(m, k), mate_rows[starts[k]:starts[k] + sizes[k]], mine, weight_mate[k]]
        sources = [own, low[0], low[1], low_last[part], high[0], high[1], high_last[part]]
        begin = [part * half] * len(sources)
        begin[3] = begin[6] = 0
        merged.append(merge_rows(place, slots, sources, begin, grads, held))
        place = after(place, merged[-1])
    far = [to_copy(mine, 2) for mine in merged]
    near = after(merged[0], merged[1])
    came = after(far[0], merged[1])
    whole = None
    for part in range(2):
        if part == 1:
            near, came = merged[1], after(far[1], whole)
        pieces = [merged[part], to_copy(near, 1), far[part], to_copy(came, 1)]
        where = [(m ^ flip) * share + part * half for flip in range(copies)]
        whole = place_rows(rows, pieces, where, whole)
    return whole


def solution(mesh):
    placed = (P("mp", "fsdp", None), P("mp", "fsdp", None), P("mp", "fsdp"), P("mp", "fsdp", None))
    return jax.shard_map(
        per_device, mesh=mesh, in_specs=placed, out_specs=P("fsdp", None), check_vma=False
    )
```

```python
import functools

import jax
import jax.numpy as jnp
from jax import lax
from jax.experimental import pallas as pl
from jax.experimental.pallas import tpu as pltpu
from jax.sharding import PartitionSpec as P

F = 7168
SEQS = 2
CHUNKS = (3, 5, 4, 4)
FLAG_ROWS = 16
COL_TILE = 256

smoothing = 0.05


def merge_kernel(copies, shards, starts, sizes, place_ref, slot_ref, *refs):
    count = 2 * shards - 1
    sources, refs = refs[:count], refs[count:]
    grads = refs[:copies]
    weights, (out_ref, acts, sem) = refs[copies:-3], refs[-3:]
    rows = acts.shape[2]
    tok = sources[0].shape[2]
    spread = sources[0].shape[0] // copies
    a, m, h = place_ref[0], place_ref[1], place_ref[2]

    def fetch(n, slot):
        for copy in range(copies):
            for part in range(spread):
                pltpu.make_async_copy(
                    sources[n].at[
                        lax.bitwise_xor(m, copy) * spread + lax.rem(h + spread - part, spread),
                        pl.ds(starts[n], rows),
                        :,
                    ],
                    acts.at[copy, slot, :, pl.ds(part * tok, tok)],
                    sem,
                ).start()

    @pl.when(pl.program_id(0) == 0)
    def _():
        fetch(0, 0)
        for slot in range(1, shards):
            @pl.when(a >= slot)
            def _(slot=slot):
                fetch(slot, slot)

            @pl.when(a < slot)
            def _(slot=slot):
                fetch(2 * shards - 1 - slot, slot)
        pltpu.make_async_copy(acts, acts, sem).wait()

    first = 0
    for piece, size in enumerate(sizes):
        at = slice(first, first + size)
        numer = denom = None
        for copy in range(copies):
            sums = []
            lone = slot_ref[copy]
            for offset, count in ((0, 1), (1, shards - 1)):
                total = None
                for n in range(offset, offset + count):
                    slot = lax.rem(lone + n, shards)
                    term = jnp.dot(
                        acts[copy, slot, at, :], grads[copy][slot], preferred_element_type=jnp.float32
                    )
                    total = term if total is None else total + term
                sums.append(total)
            prior = (sums[0] * sums[0] + sums[1] * sums[1]) * (1.0 / SEQS) + smoothing
            term = prior * weights[piece * copies + copy][...].astype(jnp.float32)
            numer = term if numer is None else numer + term
            denom = prior if denom is None else denom + prior
        out_ref[at, :] = (numer / denom).astype(out_ref.dtype)
        first += size


def merge_rows(place, slots, sources, starts, grads, weights):
    copies, shards = len(grads), grads[0].shape[0]
    tok, width = grads[0].shape[1:]
    sizes = [piece.shape[0] for piece in weights[::copies]]
    rows = sum(sizes)
    return pl.pallas_call(
        functools.partial(merge_kernel, copies, shards, starts, sizes),
        out_shape=jax.ShapeDtypeStruct((rows, width), jnp.bfloat16),
        grid_spec=pltpu.PrefetchScalarGridSpec(
            num_scalar_prefetch=2,
            grid=(width // COL_TILE,),
            in_specs=[pl.BlockSpec(memory_space=pl.ANY)] * len(sources)
            + [pl.BlockSpec((shards, tok, COL_TILE), lambda j, *_: (0, 0, j))] * copies
            + [pl.BlockSpec((piece.shape[0], COL_TILE), lambda j, *_: (0, j)) for piece in weights],
            out_specs=pl.BlockSpec((rows, COL_TILE), lambda j, *_: (0, j)),
            scratch_shapes=[
                pltpu.VMEM((copies, shards, rows, tok), jnp.bfloat16),
                pltpu.SemaphoreType.DMA,
            ],
        ),
        compiler_params=pltpu.CompilerParams(vmem_limit_bytes=56 * 1024 * 1024),
        cost_estimate=pl.CostEstimate(
            flops=2 * copies * shards * tok * rows * width, bytes_accessed=2 * copies * shards * tok * width, transcendentals=0
        ),
    )(place, slots, *sources, *grads, *weights)


def place_kernel(count, where_ref, *refs):
    pieces, (out_ref, sems) = refs[:count], refs[-2:]
    moves = [
        pltpu.make_async_copy(
            piece,
            out_ref.at[pl.ds(pl.multiple_of(where_ref[n], 16), piece.shape[0]), :],
            sems.at[n],
        )
        for n, piece in enumerate(pieces)
    ]
    for move in moves:
        move.start()
    for move in moves:
        move.wait()


def place_rows(total, pieces, where, whole):
    count = len(pieces)
    shape = jax.ShapeDtypeStruct((total, pieces[0].shape[1]), pieces[0].dtype)
    more = [] if whole is None else [whole]
    return pl.pallas_call(
        functools.partial(place_kernel, count),
        out_shape=shape,
        grid_spec=pltpu.PrefetchScalarGridSpec(
            num_scalar_prefetch=1,
            grid=(1,),
            in_specs=[pl.BlockSpec(piece.shape, lambda *_: (0, 0)) for piece in pieces]
            + [pl.BlockSpec(memory_space=pl.ANY)] * len(more),
            out_specs=pl.BlockSpec(memory_space=pl.ANY),
            scratch_shapes=[pltpu.SemaphoreType.DMA((count,))],
        ),
        input_output_aliases={1 + count: 0} if more else {},
        compiler_params=pltpu.CompilerParams(vmem_limit_bytes=32 * 1024 * 1024),
        cost_estimate=pl.CostEstimate(
            flops=0, bytes_accessed=4 * sum(p.size for p in pieces), transcendentals=0
        ),
    )(jnp.stack(where).astype(jnp.int32), *pieces, *more)


def after(value, *others):
    return lax.optimization_barrier((value, *others))[0]


def per_device(activations, out_grads, seq_ids, weights):
    copies = lax.axis_size("mp")
    devices = lax.axis_size("fsdp")
    rows, width = weights.shape[1:]
    blocks = F // width
    spread = devices // blocks
    tok = activations.shape[1]
    share = rows // copies
    sizes = [share * n // sum(CHUNKS) for n in CHUNKS]
    starts = [sum(sizes[:k]) for k in range(len(sizes))]
    m = lax.axis_index("mp")
    i = lax.axis_index("fsdp")
    a, h = i // spread, i % spread
    chip, core = m // 2, m % 2

    def to_copy(value, flip):
        return lax.ppermute(value, "mp", [(s, s ^ flip) for s in range(copies)])

    def to_block(value, shift):
        pairs = [(s, (s // spread + shift) % blocks * spread + s % spread) for s in range(devices)]
        return lax.ppermute(value, "fsdp", pairs)

    def to_half(value, shift):
        pairs = [(s, s // spread * spread + (s % spread + shift) % spread) for s in range(devices)]
        return lax.ppermute(value, "fsdp", pairs)

    def along(value, step, direction):
        pairs = [
            (s, s + direction * spread)
            for s in range(devices)
            if 0 <= s // spread + direction < blocks and 0 <= s // spread - direction * (step - 1) < blocks
        ]
        return lax.ppermute(value, "fsdp", pairs)

    def cut_blocks(value):
        return [lax.dynamic_slice_in_dim(value, (a + k) % blocks * width, width, 1) for k in range(blocks)]

    def spread_blocks(cut):
        return jnp.stack([cut[0]] + [to_block(cut[k], k) for k in range(1, blocks)])

    def over_halves(value):
        return jnp.concatenate([value] + [to_half(value, d) for d in range(1, spread)], axis=1)

    def weight_rows(owner, k):
        return lax.dynamic_slice_in_dim(weights[0], owner * share + starts[k], sizes[k], 0)

    def mate(value, *others):
        return to_copy(after(value, *others), 1)

    cut = cut_blocks(out_grads[0])
    grad_near = spread_blocks(cut)
    acts = after(activations[0], *cut).T.reshape(spread, copies, share, tok).transpose(1, 0, 2, 3)
    named = jnp.broadcast_to(seq_ids[0].astype(acts.dtype), acts.shape[:2] + (FLAG_ROWS, tok))
    acts = jnp.concatenate([acts, named], axis=2).reshape(copies * spread, share + FLAG_ROWS, tok)
    grad_far = to_copy(after(out_grads[0], acts), 2)
    planes = [
        [c * devices + block * spread + s for c in range(copies) for s in range(spread)] for block in range(blocks)
    ]
    own = lax.all_to_all(acts, ("mp", "fsdp"), 0, 0, axis_index_groups=planes, tiled=True)
    leaving = [jnp.stack([weight_rows((1 - chip) * 2 + c, k) for c in range(2)]) for k in range(len(sizes))]
    owner = after(chip * 2 + 1 - core, acts)
    mate_rows = to_copy(lax.dynamic_slice_in_dim(weights[0], owner * share, share, 0), 1)

    weight_far = [None] * len(sizes)
    weight_mate = [None] * len(sizes)

    def send_weights(k, *others):
        weight_far[k] = to_copy(after(leaving[k], *others), 2)

    def cores(k, *others):
        other = after(1 - core, *others)
        weight_mate[k] = to_copy(lax.dynamic_index_in_dim(weight_far[k], other, 0, keepdims=False), 1)

    grads = [None] * copies
    stage = (own, grad_near, *leaving)
    early = stage
    low, high = [along(after(own, *stage), 1, 1)], [along(after(own, *stage), 1, -1)]
    send_weights(0, *stage, grad_far)
    grads[0] = over_halves(after(grad_near, *stage))

    send_weights(1, *early)
    cut = cut_blocks(grad_far)
    stage = (low[0], high[0], grads[0], mate_rows, weight_far[0], *cut)
    early = stage
    grad_far = spread_blocks([after(block, *stage) for block in cut])
    grads[1] = mate(grads[0], *stage)

    stage = (grad_far, grads[1])
    low.append(along(after(low[0], *stage), 2, 1))
    high.append(along(after(high[0], *stage), 2, -1))
    send_weights(2, *early)
    early = stage
    grads[2] = over_halves(after(grad_far, *stage))
    cores(0, *stage)
    cores(1, weight_mate[0])
    named = jnp.where(a == 0, high[0][:, share, 0], jnp.where(a == blocks - 1, low[0][:, share, 0], own[:, share, 0]))
    alone = jnp.where(named[::spread] > 0.5, 0, blocks - 1)[m ^ jnp.arange(copies)]
    slots = ((a - alone) % blocks).astype(jnp.int32)
    place = jnp.stack([a, m, h]).astype(jnp.int32)

    stage = (low[1], high[1], weight_far[2], grads[1], grads[2], weight_mate[1], slots)
    half = starts[2]
    grads[3] = mate(grads[2], *stage)
    low_last = [along(after(low[1], *stage)[:, :half], 3, 1)]
    high_last = [along(after(high[1], *stage)[:, :half], 3, -1)]
    low_last.append(along(after(low[1], *stage)[:, half:share], 3, 1))
    high_last.append(along(after(high[1], *stage)[:, half:share], 3, -1))
    cores(2, *stage, grads[3])
    send_weights(3, *early)

    def sums(part, pieces, place, *others):
        held = []
        for k in pieces:
            mine = lax.dynamic_index_in_dim(weight_far[k], after(core, *others), 0, keepdims=False)
            held += [weight_rows(m, k), mate_rows[starts[k]:starts[k] + sizes[k]], mine, weight_mate[k]]
        sources = [own, low[0], low[1], low_last[part], high[0], high[1], high_last[part]]
        begin = [part * half] * len(sources)
        begin[3] = begin[6] = 0
        return merge_rows(place, slots, sources, begin, grads, held)

    where = [[(m ^ flip) * share + part * half for flip in range(copies)] for part in range(2)]
    first = sums(0, (0, 1), place)
    far_first = to_copy(first, 2)
    cores(3, first)
    second = sums(1, (2, 3), after(place, first), first)
    far_second = to_copy(second, 2)
    near_first = to_copy(after(first, second), 1)
    near_second = to_copy(second, 1)
    mate_first = to_copy(after(far_first, second), 1)
    pieces = [first, near_first, far_first, mate_first, second, near_second]
    whole = place_rows(rows, pieces, where[0] + where[1][:2], None)
    mate_second = to_copy(after(far_second, whole), 1)
    whole = place_rows(rows, [far_second], where[1][2:3], whole)
    return place_rows(rows, [mate_second], where[1][3:], whole)


def solution(mesh):
    placed = (P("mp", "fsdp", None), P("mp", "fsdp", None), P("mp", "fsdp"), P("mp", "fsdp", None))
    return jax.shard_map(
        per_device, mesh=mesh, in_specs=placed, out_specs=P("fsdp", None), check_vma=False
    )
```

```python
import functools

import jax
import jax.numpy as jnp
from jax import lax
from jax.experimental import pallas as pl
from jax.experimental.pallas import tpu as pltpu
from jax.sharding import PartitionSpec as P

F = 7168
SEQS = 2
CHUNKS = (1, 5, 5, 5)
FLAG_ROWS = 16
COL_TILE = 256

smoothing = 0.05


def merge_kernel(copies, shards, starts, sizes, place_ref, slot_ref, *refs):
    count = 2 * shards - 1
    sources, refs = refs[:count], refs[count:]
    grads = refs[:copies]
    weights, (out_ref, acts, sem) = refs[copies:-3], refs[-3:]
    rows = acts.shape[2]
    tok = sources[0].shape[2]
    spread = sources[0].shape[0] // copies
    a, m, h = place_ref[0], place_ref[1], place_ref[2]

    def fetch(n, slot):
        for copy in range(copies):
            for part in range(spread):
                pltpu.make_async_copy(
                    sources[n].at[
                        lax.bitwise_xor(m, copy) * spread + lax.rem(h + spread - part, spread),
                        pl.ds(starts[n], rows),
                        :,
                    ],
                    acts.at[copy, slot, :, pl.ds(part * tok, tok)],
                    sem,
                ).start()

    @pl.when(pl.program_id(0) == 0)
    def _():
        fetch(0, 0)
        for slot in range(1, shards):
            @pl.when(a >= slot)
            def _(slot=slot):
                fetch(slot, slot)

            @pl.when(a < slot)
            def _(slot=slot):
                fetch(2 * shards - 1 - slot, slot)
        pltpu.make_async_copy(acts, acts, sem).wait()

    first = 0
    for piece, size in enumerate(sizes):
        at = slice(first, first + size)
        numer = denom = None
        for copy in range(copies):
            sums = []
            lone = slot_ref[copy]
            for offset, count in ((0, 1), (1, shards - 1)):
                total = None
                for n in range(offset, offset + count):
                    slot = lax.rem(lone + n, shards)
                    term = jnp.dot(
                        acts[copy, slot, at, :], grads[copy][slot], preferred_element_type=jnp.float32
                    )
                    total = term if total is None else total + term
                sums.append(total)
            prior = (sums[0] * sums[0] + sums[1] * sums[1]) * (1.0 / SEQS) + smoothing
            term = prior * weights[piece * copies + copy][...].astype(jnp.float32)
            numer = term if numer is None else numer + term
            denom = prior if denom is None else denom + prior
        out_ref[at, :] = (numer / denom).astype(out_ref.dtype)
        first += size


def merge_rows(place, slots, sources, starts, grads, weights):
    copies, shards = len(grads), grads[0].shape[0]
    tok, width = grads[0].shape[1:]
    sizes = [piece.shape[0] for piece in weights[::copies]]
    rows = sum(sizes)
    return pl.pallas_call(
        functools.partial(merge_kernel, copies, shards, starts, sizes),
        out_shape=jax.ShapeDtypeStruct((rows, width), jnp.bfloat16),
        grid_spec=pltpu.PrefetchScalarGridSpec(
            num_scalar_prefetch=2,
            grid=(width // COL_TILE,),
            in_specs=[pl.BlockSpec(memory_space=pl.ANY)] * len(sources)
            + [pl.BlockSpec((shards, tok, COL_TILE), lambda j, *_: (0, 0, j))] * copies
            + [pl.BlockSpec((piece.shape[0], COL_TILE), lambda j, *_: (0, j)) for piece in weights],
            out_specs=pl.BlockSpec((rows, COL_TILE), lambda j, *_: (0, j)),
            scratch_shapes=[
                pltpu.VMEM((copies, shards, rows, tok), jnp.bfloat16),
                pltpu.SemaphoreType.DMA,
            ],
        ),
        compiler_params=pltpu.CompilerParams(vmem_limit_bytes=56 * 1024 * 1024),
        cost_estimate=pl.CostEstimate(
            flops=2 * copies * shards * tok * rows * width, bytes_accessed=2 * copies * shards * tok * width, transcendentals=0
        ),
    )(place, slots, *sources, *grads, *weights)


def place_kernel(count, where_ref, *refs):
    pieces, (out_ref, sems) = refs[:count], refs[-2:]
    moves = [
        pltpu.make_async_copy(
            piece,
            out_ref.at[pl.ds(pl.multiple_of(where_ref[n], 16), piece.shape[0]), :],
            sems.at[n],
        )
        for n, piece in enumerate(pieces)
    ]
    for move in moves:
        move.start()
    for move in moves:
        move.wait()


def place_rows(total, pieces, where, whole):
    count = len(pieces)
    shape = jax.ShapeDtypeStruct((total, pieces[0].shape[1]), pieces[0].dtype)
    more = [] if whole is None else [whole]
    return pl.pallas_call(
        functools.partial(place_kernel, count),
        out_shape=shape,
        grid_spec=pltpu.PrefetchScalarGridSpec(
            num_scalar_prefetch=1,
            grid=(1,),
            in_specs=[pl.BlockSpec(piece.shape, lambda *_: (0, 0)) for piece in pieces]
            + [pl.BlockSpec(memory_space=pl.ANY)] * len(more),
            out_specs=pl.BlockSpec(memory_space=pl.ANY),
            scratch_shapes=[pltpu.SemaphoreType.DMA((count,))],
        ),
        input_output_aliases={1 + count: 0} if more else {},
        compiler_params=pltpu.CompilerParams(vmem_limit_bytes=32 * 1024 * 1024),
        cost_estimate=pl.CostEstimate(
            flops=0, bytes_accessed=4 * sum(p.size for p in pieces), transcendentals=0
        ),
    )(jnp.stack(where).astype(jnp.int32), *pieces, *more)


def prepare_kernel(acts_ref, owner_ref, out_ref):
    share = acts_ref.shape[1]
    out_ref[0, :share, :] = acts_ref[...].T
    named = owner_ref[...].astype(jnp.float32).astype(out_ref.dtype)
    out_ref[0, share:, :] = jnp.broadcast_to(named, (FLAG_ROWS, named.shape[1]))


def prepare(acts, owners, copies, spread):
    tok, features = acts.shape
    share = features // (copies * spread)
    return pl.pallas_call(
        prepare_kernel,
        out_shape=jax.ShapeDtypeStruct((copies * spread, share + FLAG_ROWS, tok), acts.dtype),
        grid=(copies * spread,),
        in_specs=[
            pl.BlockSpec((tok, share), lambda p: (0, p % spread * copies + p // spread)),
            pl.BlockSpec((1, tok), lambda p: (0, 0)),
        ],
        out_specs=pl.BlockSpec((1, share + FLAG_ROWS, tok), lambda p: (p, 0, 0)),
        compiler_params=pltpu.CompilerParams(vmem_limit_bytes=16 * 1024 * 1024),
        cost_estimate=pl.CostEstimate(flops=0, bytes_accessed=4 * acts.size, transcendentals=0),
    )(acts, owners)


def after(value, *others):
    return lax.optimization_barrier((value, *others))[0]


def per_device(activations, out_grads, seq_ids, weights):
    copies = lax.axis_size("mp")
    devices = lax.axis_size("fsdp")
    rows, width = weights.shape[1:]
    blocks = F // width
    spread = devices // blocks
    tok = activations.shape[1]
    share = rows // copies
    sizes = [share * n // sum(CHUNKS) for n in CHUNKS]
    starts = [sum(sizes[:k]) for k in range(len(sizes))]
    m = lax.axis_index("mp")
    i = lax.axis_index("fsdp")
    a, h = i // spread, i % spread
    chip, core = m // 2, m % 2

    def to_copy(value, flip):
        return lax.ppermute(value, "mp", [(s, s ^ flip) for s in range(copies)])

    def to_block(value, shift):
        pairs = [(s, (s // spread + shift) % blocks * spread + s % spread) for s in range(devices)]
        return lax.ppermute(value, "fsdp", pairs)

    def to_half(value, shift):
        pairs = [(s, s // spread * spread + (s % spread + shift) % spread) for s in range(devices)]
        return lax.ppermute(value, "fsdp", pairs)

    def along(value, step, direction):
        pairs = [
            (s, s + direction * spread)
            for s in range(devices)
            if 0 <= s // spread + direction < blocks and 0 <= s // spread - direction * (step - 1) < blocks
        ]
        return lax.ppermute(value, "fsdp", pairs)

    def cut_blocks(value):
        return [lax.dynamic_slice_in_dim(value, (a + k) % blocks * width, width, 1) for k in range(blocks)]

    def spread_blocks(cut):
        return jnp.stack([cut[0]] + [to_block(cut[k], k) for k in range(1, blocks)])

    def over_halves(value):
        return jnp.concatenate([value] + [to_half(value, d) for d in range(1, spread)], axis=1)

    def weight_rows(owner, k):
        return lax.dynamic_slice_in_dim(weights[0], owner * share + starts[k], sizes[k], 0)

    def mate(value, *others):
        return to_copy(after(value, *others), 1)

    cut = cut_blocks(out_grads[0])
    grad_near = spread_blocks(cut)
    acts = prepare(after(activations[0], *cut), seq_ids, copies, spread)
    grad_far = to_copy(after(out_grads[0], acts), 2)
    planes = [
        [c * devices + block * spread + s for c in range(copies) for s in range(spread)] for block in range(blocks)
    ]
    own = lax.all_to_all(acts, ("mp", "fsdp"), 0, 0, axis_index_groups=planes, tiled=True)
    leaving = [jnp.stack([weight_rows((1 - chip) * 2 + c, k) for c in range(2)]) for k in range(len(sizes))]
    owner = after(chip * 2 + 1 - core, acts)
    mate_rows = to_copy(lax.dynamic_slice_in_dim(weights[0], owner * share, share, 0), 1)

    weight_far = [None] * len(sizes)
    weight_mate = [None] * len(sizes)

    def send_weights(k, *others):
        weight_far[k] = to_copy(after(leaving[k], *others), 2)

    def cores(k, *others):
        other = after(1 - core, *others)
        weight_mate[k] = to_copy(lax.dynamic_index_in_dim(weight_far[k], other, 0, keepdims=False), 1)

    grads = [None] * copies
    stage = (own, grad_near, *leaving)
    early = stage
    low, high = [along(after(own, *stage), 1, 1)], [along(after(own, *stage), 1, -1)]
    send_weights(0, *stage, grad_far)
    grads[0] = over_halves(after(grad_near, *stage))

    send_weights(1, *early)
    cut = cut_blocks(grad_far)
    stage = (low[0], high[0], grads[0], mate_rows, weight_far[0], *cut)
    early = stage
    grad_far = spread_blocks([after(block, *stage) for block in cut])
    grads[1] = mate(grads[0], *stage)

    stage = (grad_far, grads[1], weight_far[1])
    low.append(along(after(low[0], *stage), 2, 1))
    high.append(along(after(high[0], *stage), 2, -1))
    send_weights(2, *early)
    early = stage
    grads[2] = over_halves(after(grad_far, *stage))
    cores(0, *stage)
    cores(1, weight_mate[0])
    named = jnp.where(a == 0, high[0][:, share, 0], jnp.where(a == blocks - 1, low[0][:, share, 0], own[:, share, 0]))
    alone = jnp.where(named[::spread] > 0.5, 0, blocks - 1)[m ^ jnp.arange(copies)]
    slots = ((a - alone) % blocks).astype(jnp.int32)
    place = jnp.stack([a, m, h]).astype(jnp.int32)

    stage = (low[1], high[1], weight_far[2], grads[1], grads[2], weight_mate[1], slots)
    half = starts[2]
    grads[3] = mate(grads[2], *stage)
    low_last = [along(after(low[1], *stage)[:, :half], 3, 1)]
    high_last = [along(after(high[1], *stage)[:, :half], 3, -1)]
    low_last.append(along(after(low[1], *stage)[:, half:share], 3, 1))
    high_last.append(along(after(high[1], *stage)[:, half:share], 3, -1))
    cores(2, *stage, grads[3])
    send_weights(3, *early)

    def sums(part, pieces, place, *others):
        held = []
        for k in pieces:
            mine = lax.dynamic_index_in_dim(weight_far[k], after(core, *others), 0, keepdims=False)
            held += [weight_rows(m, k), mate_rows[starts[k]:starts[k] + sizes[k]], mine, weight_mate[k]]
        sources = [own, low[0], low[1], low_last[part], high[0], high[1], high_last[part]]
        begin = [part * half] * len(sources)
        begin[3] = begin[6] = 0
        return merge_rows(place, slots, sources, begin, grads, held)

    where = [[(m ^ flip) * share + part * half for flip in range(copies)] for part in range(2)]
    first = sums(0, (0, 1), place)
    far_first = to_copy(first, 2)
    cores(3, first)
    second = sums(1, (2, 3), after(place, first), first)
    far_second = to_copy(second, 2)
    near_first = to_copy(after(first, second), 1)
    near_second = to_copy(second, 1)
    mate_first = to_copy(after(far_first, second), 1)
    pieces = [first, near_first, far_first, mate_first, second, near_second]
    whole = place_rows(rows, pieces, where[0] + where[1][:2], None)
    mate_second = to_copy(after(far_second, whole), 1)
    whole = place_rows(rows, [far_second], where[1][2:3], whole)
    return place_rows(rows, [mate_second], where[1][3:], whole)


def solution(mesh):
    placed = (P("mp", "fsdp", None), P("mp", "fsdp", None), P("mp", "fsdp"), P("mp", "fsdp", None))
    return jax.shard_map(
        per_device, mesh=mesh, in_specs=placed, out_specs=P("fsdp", None), check_vma=False
    )
```

```python
import functools

import jax
import jax.numpy as jnp
from jax import lax
from jax.experimental import pallas as pl
from jax.experimental.pallas import tpu as pltpu
from jax.sharding import PartitionSpec as P

F = 7168
SEQS = 2
CHUNKS = (2, 5, 5, 4)
FLAG_ROWS = 16
COL_TILE = 256

smoothing = 0.05


def merge_kernel(copies, shards, starts, sizes, place_ref, slot_ref, *refs):
    count = 2 * shards - 1
    sources, refs = refs[:count], refs[count:]
    grads = refs[:copies]
    weights, (out_ref, acts, sem) = refs[copies:-3], refs[-3:]
    rows = acts.shape[2]
    tok = sources[0].shape[2]
    spread = sources[0].shape[0] // copies
    a, m, h = place_ref[0], place_ref[1], place_ref[2]

    def fetch(n, slot):
        for copy in range(copies):
            for part in range(spread):
                pltpu.make_async_copy(
                    sources[n].at[
                        lax.bitwise_xor(m, copy) * spread + lax.rem(h + spread - part, spread),
                        pl.ds(starts[n], rows),
                        :,
                    ],
                    acts.at[copy, slot, :, pl.ds(part * tok, tok)],
                    sem,
                ).start()

    @pl.when(pl.program_id(0) == 0)
    def _():
        fetch(0, 0)
        for slot in range(1, shards):
            @pl.when(a >= slot)
            def _(slot=slot):
                fetch(slot, slot)

            @pl.when(a < slot)
            def _(slot=slot):
                fetch(2 * shards - 1 - slot, slot)
        pltpu.make_async_copy(acts, acts, sem).wait()

    first = 0
    for piece, size in enumerate(sizes):
        at = slice(first, first + size)
        numer = denom = None
        for copy in range(copies):
            sums = []
            lone = slot_ref[copy]
            for offset, count in ((0, 1), (1, shards - 1)):
                total = None
                for n in range(offset, offset + count):
                    slot = lax.rem(lone + n, shards)
                    term = jnp.dot(
                        acts[copy, slot, at, :], grads[copy][slot], preferred_element_type=jnp.float32
                    )
                    total = term if total is None else total + term
                sums.append(total)
            prior = (sums[0] * sums[0] + sums[1] * sums[1]) * (1.0 / SEQS) + smoothing
            term = prior * weights[piece * copies + copy][...].astype(jnp.float32)
            numer = term if numer is None else numer + term
            denom = prior if denom is None else denom + prior
        out_ref[at, :] = (numer / denom).astype(out_ref.dtype)
        first += size


def merge_rows(place, slots, sources, starts, grads, weights):
    copies, shards = len(grads), grads[0].shape[0]
    tok, width = grads[0].shape[1:]
    sizes = [piece.shape[0] for piece in weights[::copies]]
    rows = sum(sizes)
    return pl.pallas_call(
        functools.partial(merge_kernel, copies, shards, starts, sizes),
        out_shape=jax.ShapeDtypeStruct((rows, width), jnp.bfloat16),
        grid_spec=pltpu.PrefetchScalarGridSpec(
            num_scalar_prefetch=2,
            grid=(width // COL_TILE,),
            in_specs=[pl.BlockSpec(memory_space=pl.ANY)] * len(sources)
            + [pl.BlockSpec((shards, tok, COL_TILE), lambda j, *_: (0, 0, j))] * copies
            + [pl.BlockSpec((piece.shape[0], COL_TILE), lambda j, *_: (0, j)) for piece in weights],
            out_specs=pl.BlockSpec((rows, COL_TILE), lambda j, *_: (0, j)),
            scratch_shapes=[
                pltpu.VMEM((copies, shards, rows, tok), jnp.bfloat16),
                pltpu.SemaphoreType.DMA,
            ],
        ),
        compiler_params=pltpu.CompilerParams(vmem_limit_bytes=56 * 1024 * 1024),
        cost_estimate=pl.CostEstimate(
            flops=2 * copies * shards * tok * rows * width, bytes_accessed=2 * copies * shards * tok * width, transcendentals=0
        ),
    )(place, slots, *sources, *grads, *weights)


def place_kernel(count, where_ref, *refs):
    pieces, (out_ref, sems) = refs[:count], refs[-2:]
    moves = [
        pltpu.make_async_copy(
            piece,
            out_ref.at[pl.ds(pl.multiple_of(where_ref[n], 16), piece.shape[0]), :],
            sems.at[n],
        )
        for n, piece in enumerate(pieces)
    ]
    for move in moves:
        move.start()
    for move in moves:
        move.wait()


def place_rows(total, pieces, where, whole):
    count = len(pieces)
    shape = jax.ShapeDtypeStruct((total, pieces[0].shape[1]), pieces[0].dtype)
    more = [] if whole is None else [whole]
    return pl.pallas_call(
        functools.partial(place_kernel, count),
        out_shape=shape,
        grid_spec=pltpu.PrefetchScalarGridSpec(
            num_scalar_prefetch=1,
            grid=(1,),
            in_specs=[pl.BlockSpec(piece.shape, lambda *_: (0, 0)) for piece in pieces]
            + [pl.BlockSpec(memory_space=pl.ANY)] * len(more),
            out_specs=pl.BlockSpec(memory_space=pl.ANY),
            scratch_shapes=[pltpu.SemaphoreType.DMA((count,))],
        ),
        input_output_aliases={1 + count: 0} if more else {},
        compiler_params=pltpu.CompilerParams(vmem_limit_bytes=32 * 1024 * 1024),
        cost_estimate=pl.CostEstimate(
            flops=0, bytes_accessed=4 * sum(p.size for p in pieces), transcendentals=0
        ),
    )(jnp.stack(where).astype(jnp.int32), *pieces, *more)


def prepare_kernel(acts_ref, owner_ref, out_ref):
    share = acts_ref.shape[1]
    out_ref[0, :share, :] = acts_ref[...].T
    named = owner_ref[...].astype(jnp.float32).astype(out_ref.dtype)
    out_ref[0, share:, :] = jnp.broadcast_to(named, (FLAG_ROWS, named.shape[1]))


def prepare(acts, owners, copies, spread):
    tok, features = acts.shape
    share = features // (copies * spread)
    return pl.pallas_call(
        prepare_kernel,
        out_shape=jax.ShapeDtypeStruct((copies * spread, share + FLAG_ROWS, tok), acts.dtype),
        grid=(copies * spread,),
        in_specs=[
            pl.BlockSpec((tok, share), lambda p: (0, p % spread * copies + p // spread)),
            pl.BlockSpec((1, tok), lambda p: (0, 0)),
        ],
        out_specs=pl.BlockSpec((1, share + FLAG_ROWS, tok), lambda p: (p, 0, 0)),
        compiler_params=pltpu.CompilerParams(vmem_limit_bytes=16 * 1024 * 1024),
        cost_estimate=pl.CostEstimate(flops=0, bytes_accessed=4 * acts.size, transcendentals=0),
    )(acts, owners)


def after(value, *others):
    return lax.optimization_barrier((value, *others))[0]


def per_device(activations, out_grads, seq_ids, weights):
    copies = lax.axis_size("mp")
    devices = lax.axis_size("fsdp")
    rows, width = weights.shape[1:]
    blocks = F // width
    spread = devices // blocks
    tok = activations.shape[1]
    share = rows // copies
    sizes = [share * n // sum(CHUNKS) for n in CHUNKS]
    starts = [sum(sizes[:k]) for k in range(len(sizes))]
    m = lax.axis_index("mp")
    i = lax.axis_index("fsdp")
    a, h = i // spread, i % spread
    chip, core = m // 2, m % 2

    def to_copy(value, flip):
        return lax.ppermute(value, "mp", [(s, s ^ flip) for s in range(copies)])

    def to_block(value, shift):
        pairs = [(s, (s // spread + shift) % blocks * spread + s % spread) for s in range(devices)]
        return lax.ppermute(value, "fsdp", pairs)

    def to_half(value, shift):
        pairs = [(s, s // spread * spread + (s % spread + shift) % spread) for s in range(devices)]
        return lax.ppermute(value, "fsdp", pairs)

    def along(value, step, direction):
        pairs = [
            (s, s + direction * spread)
            for s in range(devices)
            if 0 <= s // spread + direction < blocks and 0 <= s // spread - direction * (step - 1) < blocks
        ]
        return lax.ppermute(value, "fsdp", pairs)

    def cut_blocks(value):
        return [lax.dynamic_slice_in_dim(value, (a + k) % blocks * width, width, 1) for k in range(blocks)]

    def spread_blocks(cut):
        return [cut[0]] + [to_block(cut[k], k) for k in range(1, blocks)]

    def over_halves(value):
        return [value] + [to_half(value, d) for d in range(1, spread)]

    def weight_rows(owner, k):
        return lax.dynamic_slice_in_dim(weights[0], owner * share + starts[k], sizes[k], 0)

    def mate(value, *others):
        return to_copy(after(value, *others), 1)

    cut = cut_blocks(out_grads[0])
    grad_near = spread_blocks(cut)
    acts = prepare(after(activations[0], *cut), seq_ids, copies, spread)
    grad_far = to_copy(after(out_grads[0], acts), 2)
    planes = [
        [c * devices + block * spread + s for c in range(copies) for s in range(spread)] for block in range(blocks)
    ]
    own = lax.all_to_all(acts, ("mp", "fsdp"), 0, 0, axis_index_groups=planes, tiled=True)
    leaving = [jnp.stack([weight_rows((1 - chip) * 2 + c, k) for c in range(2)]) for k in range(len(sizes))]
    owner = after(chip * 2 + 1 - core, acts)
    mate_rows = to_copy(lax.dynamic_slice_in_dim(weights[0], owner * share, share, 0), 1)

    weight_far = [None] * len(sizes)
    weight_mate = [None] * len(sizes)

    def send_weights(k, *others):
        weight_far[k] = to_copy(after(leaving[k], *others), 2)

    def cores(k, *others):
        other = after(1 - core, *others)
        weight_mate[k] = to_copy(lax.dynamic_index_in_dim(weight_far[k], other, 0, keepdims=False), 1)

    grads = [None] * copies
    stage = (own, *grad_near, *leaving)
    early = stage
    low, high = [along(after(own, *stage), 1, 1)], [along(after(own, *stage), 1, -1)]
    send_weights(0, *stage, grad_far)
    halves = over_halves(after(jnp.stack(grad_near), *stage))
    grads[0] = jnp.concatenate(halves, axis=1)

    send_weights(1, *early)
    cut = cut_blocks(grad_far)
    stage = (low[0], high[0], *halves, mate_rows, weight_far[0], *cut)
    early = stage
    grad_far = spread_blocks([after(block, *stage) for block in cut])
    grads[1] = mate(grads[0], *stage)

    stage = (*grad_far, grads[1], weight_far[1])
    low.append(along(after(low[0], *stage), 2, 1))
    high.append(along(after(high[0], *stage), 2, -1))
    send_weights(2, *early)
    early = stage
    halves = over_halves(after(jnp.stack(grad_far), *stage))
    grads[2] = jnp.concatenate(halves, axis=1)
    cores(0, *stage)
    cores(1, weight_mate[0])
    named = jnp.where(a == 0, high[0][:, share, 0], jnp.where(a == blocks - 1, low[0][:, share, 0], own[:, share, 0]))
    alone = jnp.where(named[::spread] > 0.5, 0, blocks - 1)[m ^ jnp.arange(copies)]
    slots = ((a - alone) % blocks).astype(jnp.int32)
    place = jnp.stack([a, m, h]).astype(jnp.int32)

    stage = (low[1], high[1], weight_far[2], grads[1], *halves, weight_mate[1], slots)
    half = starts[2]
    grads[3] = mate(grads[2], *stage)
    low_last = [along(after(low[1], *stage)[:, :half], 3, 1)]
    high_last = [along(after(high[1], *stage)[:, :half], 3, -1)]
    low_last.append(along(after(low[1], *stage)[:, half:share], 3, 1))
    high_last.append(along(after(high[1], *stage)[:, half:share], 3, -1))
    cores(2, *stage, grads[3])
    send_weights(3, *early)

    def sums(part, pieces, place, *others):
        held = []
        for k in pieces:
            mine = lax.dynamic_index_in_dim(weight_far[k], after(core, *others), 0, keepdims=False)
            held += [weight_rows(m, k), mate_rows[starts[k]:starts[k] + sizes[k]], mine, weight_mate[k]]
        sources = [own, low[0], low[1], low_last[part], high[0], high[1], high_last[part]]
        begin = [part * half] * len(sources)
        begin[3] = begin[6] = 0
        return merge_rows(place, slots, sources, begin, grads, held)

    where = [[(m ^ flip) * share + part * half for flip in range(copies)] for part in range(2)]
    first = sums(0, (0, 1), place)
    far_first = to_copy(first, 2)
    cores(3, first)
    second = sums(1, (2, 3), after(place, first), first)
    far_second = to_copy(second, 2)
    near_first = to_copy(after(first, second), 1)
    near_second = to_copy(second, 1)
    mate_first = to_copy(after(far_first, second), 1)
    pieces = [first, near_first, far_first, mate_first, second, near_second]
    whole = place_rows(rows, pieces, where[0] + where[1][:2], None)
    mate_second = to_copy(after(far_second, whole), 1)
    whole = place_rows(rows, [far_second], where[1][2:3], whole)
    return place_rows(rows, [mate_second], where[1][3:], whole)


def solution(mesh):
    placed = (P("mp", "fsdp", None), P("mp", "fsdp", None), P("mp", "fsdp"), P("mp", "fsdp", None))
    return jax.shard_map(
        per_device, mesh=mesh, in_specs=placed, out_specs=P("fsdp", None), check_vma=False
    )
```

```python
import functools

import jax
import jax.numpy as jnp
from jax import lax
from jax.experimental import pallas as pl
from jax.experimental.pallas import tpu as pltpu
from jax.sharding import PartitionSpec as P

F = 7168
SEQS = 2
CHUNKS = (2, 4, 6, 4)
FLAG_ROWS = 16
COL_TILE = 256

smoothing = 0.05


def merge_kernel(copies, shards, starts, sizes, place_ref, slot_ref, *refs):
    count = 2 * shards - 1
    sources, refs = refs[:count], refs[count:]
    grads = refs[:copies]
    weights, (out_ref, acts, sem) = refs[copies:-3], refs[-3:]
    rows = acts.shape[2]
    tok = sources[0].shape[2]
    spread = sources[0].shape[0] // copies
    a, m, h = place_ref[0], place_ref[1], place_ref[2]

    def fetch(n, slot):
        for copy in range(copies):
            for part in range(spread):
                pltpu.make_async_copy(
                    sources[n].at[
                        lax.bitwise_xor(m, copy) * spread + lax.rem(h + spread - part, spread),
                        pl.ds(starts[n], rows),
                        :,
                    ],
                    acts.at[copy, slot, :, pl.ds(part * tok, tok)],
                    sem,
                ).start()

    @pl.when(pl.program_id(0) == 0)
    def _():
        fetch(0, 0)
        for slot in range(1, shards):
            @pl.when(a >= slot)
            def _(slot=slot):
                fetch(slot, slot)

            @pl.when(a < slot)
            def _(slot=slot):
                fetch(2 * shards - 1 - slot, slot)
        pltpu.make_async_copy(acts, acts, sem).wait()

    first = 0
    for piece, size in enumerate(sizes):
        at = slice(first, first + size)
        numer = denom = None
        for copy in range(copies):
            sums = []
            lone = slot_ref[copy]
            for offset, count in ((0, 1), (1, shards - 1)):
                total = None
                for n in range(offset, offset + count):
                    slot = lax.rem(lone + n, shards)
                    term = jnp.dot(
                        acts[copy, slot, at, :], grads[copy][slot], preferred_element_type=jnp.float32
                    )
                    total = term if total is None else total + term
                sums.append(total)
            prior = (sums[0] * sums[0] + sums[1] * sums[1]) * (1.0 / SEQS) + smoothing
            term = prior * weights[piece * copies + copy][...].astype(jnp.float32)
            numer = term if numer is None else numer + term
            denom = prior if denom is None else denom + prior
        out_ref[at, :] = (numer / denom).astype(out_ref.dtype)
        first += size


def weight_block(piece):
    rows = piece.shape[-2]
    if piece.ndim == 2:
        return pl.BlockSpec((rows, COL_TILE), lambda j, *_: (0, j))
    return pl.BlockSpec((None, rows, COL_TILE), lambda j, place, slots: (place[3], 0, j))


def merge_rows(place, slots, sources, starts, grads, weights):
    copies, shards = len(grads), grads[0].shape[0]
    tok, width = grads[0].shape[1:]
    sizes = [piece.shape[-2] for piece in weights[::copies]]
    rows = sum(sizes)
    return pl.pallas_call(
        functools.partial(merge_kernel, copies, shards, starts, sizes),
        out_shape=jax.ShapeDtypeStruct((rows, width), jnp.bfloat16),
        grid_spec=pltpu.PrefetchScalarGridSpec(
            num_scalar_prefetch=2,
            grid=(width // COL_TILE,),
            in_specs=[pl.BlockSpec(memory_space=pl.ANY)] * len(sources)
            + [pl.BlockSpec((shards, tok, COL_TILE), lambda j, *_: (0, 0, j))] * copies
            + [weight_block(piece) for piece in weights],
            out_specs=pl.BlockSpec((rows, COL_TILE), lambda j, *_: (0, j)),
            scratch_shapes=[
                pltpu.VMEM((copies, shards, rows, tok), jnp.bfloat16),
                pltpu.SemaphoreType.DMA,
            ],
        ),
        compiler_params=pltpu.CompilerParams(vmem_limit_bytes=56 * 1024 * 1024),
        cost_estimate=pl.CostEstimate(
            flops=2 * copies * shards * tok * rows * width, bytes_accessed=2 * copies * shards * tok * width, transcendentals=0
        ),
    )(place, slots, *sources, *grads, *weights)


def place_kernel(count, where_ref, *refs):
    pieces, (out_ref, sems) = refs[:count], refs[-2:]
    moves = [
        pltpu.make_async_copy(
            piece,
            out_ref.at[pl.ds(pl.multiple_of(where_ref[n], 16), piece.shape[0]), :],
            sems.at[n],
        )
        for n, piece in enumerate(pieces)
    ]
    for move in moves:
        move.start()
    for move in moves:
        move.wait()


def place_rows(total, pieces, where, whole):
    count = len(pieces)
    shape = jax.ShapeDtypeStruct((total, pieces[0].shape[1]), pieces[0].dtype)
    more = [] if whole is None else [whole]
    return pl.pallas_call(
        functools.partial(place_kernel, count),
        out_shape=shape,
        grid_spec=pltpu.PrefetchScalarGridSpec(
            num_scalar_prefetch=1,
            grid=(1,),
            in_specs=[pl.BlockSpec(piece.shape, lambda *_: (0, 0)) for piece in pieces]
            + [pl.BlockSpec(memory_space=pl.ANY)] * len(more),
            out_specs=pl.BlockSpec(memory_space=pl.ANY),
            scratch_shapes=[pltpu.SemaphoreType.DMA((count,))],
        ),
        input_output_aliases={1 + count: 0} if more else {},
        compiler_params=pltpu.CompilerParams(vmem_limit_bytes=32 * 1024 * 1024),
        cost_estimate=pl.CostEstimate(
            flops=0, bytes_accessed=4 * sum(p.size for p in pieces), transcendentals=0
        ),
    )(jnp.stack(where).astype(jnp.int32), *pieces, *more)


def prepare_kernel(acts_ref, owner_ref, out_ref):
    share = acts_ref.shape[1]
    out_ref[0, :share, :] = acts_ref[...].T
    named = owner_ref[...].astype(jnp.float32).astype(out_ref.dtype)
    out_ref[0, share:, :] = jnp.broadcast_to(named, (FLAG_ROWS, named.shape[1]))


def prepare(acts, owners, copies, spread):
    tok, features = acts.shape
    share = features // (copies * spread)
    return pl.pallas_call(
        prepare_kernel,
        out_shape=jax.ShapeDtypeStruct((copies * spread, share + FLAG_ROWS, tok), acts.dtype),
        grid=(copies * spread,),
        in_specs=[
            pl.BlockSpec((tok, share), lambda p: (0, p % spread * copies + p // spread)),
            pl.BlockSpec((1, tok), lambda p: (0, 0)),
        ],
        out_specs=pl.BlockSpec((1, share + FLAG_ROWS, tok), lambda p: (p, 0, 0)),
        compiler_params=pltpu.CompilerParams(vmem_limit_bytes=16 * 1024 * 1024),
        cost_estimate=pl.CostEstimate(flops=0, bytes_accessed=4 * acts.size, transcendentals=0),
    )(acts, owners)


def after(value, *others):
    return lax.optimization_barrier((value, *others))[0]


def per_device(activations, out_grads, seq_ids, weights):
    copies = lax.axis_size("mp")
    devices = lax.axis_size("fsdp")
    rows, width = weights.shape[1:]
    blocks = F // width
    spread = devices // blocks
    tok = activations.shape[1]
    share = rows // copies
    sizes = [share * n // sum(CHUNKS) for n in CHUNKS]
    starts = [sum(sizes[:k]) for k in range(len(sizes))]
    m = lax.axis_index("mp")
    i = lax.axis_index("fsdp")
    a, h = i // spread, i % spread
    chip, core = m // 2, m % 2

    def to_copy(value, flip):
        return lax.ppermute(value, "mp", [(s, s ^ flip) for s in range(copies)])

    def to_block(value, shift):
        pairs = [(s, (s // spread + shift) % blocks * spread + s % spread) for s in range(devices)]
        return lax.ppermute(value, "fsdp", pairs)

    def to_half(value, shift):
        pairs = [(s, s // spread * spread + (s % spread + shift) % spread) for s in range(devices)]
        return lax.ppermute(value, "fsdp", pairs)

    def along(value, step, direction):
        pairs = [
            (s, s + direction * spread)
            for s in range(devices)
            if 0 <= s // spread + direction < blocks and 0 <= s // spread - direction * (step - 1) < blocks
        ]
        return lax.ppermute(value, "fsdp", pairs)

    def cut_blocks(value):
        return [lax.dynamic_slice_in_dim(value, (a + k) % blocks * width, width, 1) for k in range(blocks)]

    def spread_blocks(cut):
        return [cut[0]] + [to_block(cut[k], k) for k in range(1, blocks)]

    def over_halves(value):
        return [value] + [to_half(value, d) for d in range(1, spread)]

    def weight_rows(owner, k):
        return lax.dynamic_slice_in_dim(weights[0], owner * share + starts[k], sizes[k], 0)

    def mate(value, *others):
        return to_copy(after(value, *others), 1)

    cut = cut_blocks(out_grads[0])
    grad_near = spread_blocks(cut)
    acts = prepare(after(activations[0], *cut), seq_ids, copies, spread)
    grad_far = to_copy(after(out_grads[0], acts), 2)
    planes = [
        [c * devices + block * spread + s for c in range(copies) for s in range(spread)] for block in range(blocks)
    ]
    own = lax.all_to_all(acts, ("mp", "fsdp"), 0, 0, axis_index_groups=planes, tiled=True)
    leaving = [jnp.stack([weight_rows((1 - chip) * 2 + c, k) for c in range(2)]) for k in range(len(sizes))]
    owner = after(chip * 2 + 1 - core, acts)
    mate_rows = to_copy(lax.dynamic_slice_in_dim(weights[0], owner * share, share, 0), 1)

    weight_far = [None] * len(sizes)
    weight_mate = [None] * len(sizes)

    def send_weights(k, *others):
        weight_far[k] = to_copy(after(leaving[k], *others), 2)

    def cores(k, *others):
        other = after(1 - core, *others)
        weight_mate[k] = to_copy(lax.dynamic_index_in_dim(weight_far[k], other, 0, keepdims=False), 1)

    grads = [None] * copies
    stage = (own, *grad_near, *leaving)
    early = stage
    low, high = [along(after(own, *stage), 1, 1)], [along(after(own, *stage), 1, -1)]
    send_weights(0, *stage, grad_far)
    halves = over_halves(after(jnp.stack(grad_near), *stage))
    grads[0] = jnp.concatenate(halves, axis=1)

    send_weights(1, *early)
    cut = cut_blocks(grad_far)
    stage = (low[0], high[0], *halves, mate_rows, weight_far[0], *cut)
    early = stage
    grad_far = spread_blocks([after(block, *stage) for block in cut])
    grads[1] = mate(grads[0], *stage)

    stage = (*grad_far, grads[1], weight_far[1])
    low.append(along(after(low[0], *stage), 2, 1))
    high.append(along(after(high[0], *stage), 2, -1))
    send_weights(2, *early)
    early = stage
    halves = over_halves(after(jnp.stack(grad_far), *stage))
    grads[2] = jnp.concatenate(halves, axis=1)
    cores(0, *stage)
    cores(1, weight_mate[0])
    named = jnp.where(a == 0, high[0][:, share, 0], jnp.where(a == blocks - 1, low[0][:, share, 0], own[:, share, 0]))
    alone = jnp.where(named[::spread] > 0.5, 0, blocks - 1)[m ^ jnp.arange(copies)]
    slots = ((a - alone) % blocks).astype(jnp.int32)
    place = jnp.stack([a, m, h, core]).astype(jnp.int32)

    stage = (low[1], high[1], weight_far[2], grads[1], *halves, weight_mate[1], slots)
    half = starts[2]
    grads[3] = mate(grads[2], *stage)
    low_last = [along(after(low[1], *stage)[:, :half], 3, 1)]
    high_last = [along(after(high[1], *stage)[:, :half], 3, -1)]
    low_last.append(along(after(low[1], *stage)[:, half:share], 3, 1))
    high_last.append(along(after(high[1], *stage)[:, half:share], 3, -1))
    cores(2, *stage, grads[3])
    send_weights(3, *early)

    def sums(part, pieces, place):
        held = []
        for k in pieces:
            held += [*ready[k], weight_far[k], weight_mate[k]]
        sources = [own, low[0], low[1], low_last[part], high[0], high[1], high_last[part]]
        begin = [part * half] * len(sources)
        begin[3] = begin[6] = 0
        return merge_rows(place, slots, sources, begin, grads, held)

    where = [[(m ^ flip) * share + part * half for flip in range(copies)] for part in range(2)]
    ready = {k: (weight_rows(m, k), mate_rows[starts[k]:starts[k] + sizes[k]]) for k in range(len(sizes))}
    first = sums(0, (0, 1), after(place, *ready[2], *ready[3]))
    far_first = to_copy(first, 2)
    cores(3, first)
    second = sums(1, (2, 3), after(place, first))
    far_second = to_copy(second, 2)
    near_first = to_copy(after(first, second), 1)
    near_second = to_copy(second, 1)
    mate_first = to_copy(after(far_first, second), 1)
    pieces = [first, near_first, far_first, mate_first, second, near_second]
    whole = place_rows(rows, pieces, where[0] + where[1][:2], None)
    mate_second = to_copy(after(far_second, whole), 1)
    whole = place_rows(rows, [far_second], where[1][2:3], whole)
    return place_rows(rows, [mate_second], where[1][3:], whole)


def solution(mesh):
    placed = (P("mp", "fsdp", None), P("mp", "fsdp", None), P("mp", "fsdp"), P("mp", "fsdp", None))
    return jax.shard_map(
        per_device, mesh=mesh, in_specs=placed, out_specs=P("fsdp", None), check_vma=False
    )
```
